256 devices in a mesh: wide: 16 (over z, core), narrow: 16 (over x, y).
Axes of the slice: x: 4, y: 4, z: 8, core: 2. Of those that a mesh axis runs over, the one named last changes fastest.
Arguments:
- block_values: bfloat16 [16384, 128, 128], P(('wide', 'narrow')), may hold values from -6 to 6
- block_rows: int32 [16384], P(('wide', 'narrow')), may hold values from 0 to 4095, as said below
- block_cols: int32 [16384], P(('wide', 'narrow')), may hold values from 0 to 255, as said below
- block_count: int32 [256], P(('wide', 'narrow')), may hold values from 16 to 64, as said below
- test_matrix: bfloat16 [32768, 128], P(('wide', 'narrow')), may hold values from -0.3125 to 0.3125
Outputs:
- q_basis: bfloat16 [524288, 128], P(('wide', 'narrow'))
- r_factor: float32 [128, 128], replicated
- projected: float32 [32768, 128], P(('wide', 'narrow'))
The draws below stay inside these ranges and needn't reach their ends.
Inputs may be any that keep to these rules, and one draw needn't show every extreme that they name: `block_rows`: every slot of device d names a block row of its own slab, d * 16 to d * 16 + 15; its first 16 slots name each of these block rows once. `block_cols`: any block column; a (block row, block column) pair may repeat. `block_count`: slots at or past a device's count are ignored; some device has all 64 slots live.
All inputs are finite; a program needn't handle non-finite values.
Results may differ from the reference program's by a relative error of at most 0.009.
Values may be sent and summed in bfloat16 or wider, within the bound.
A program may use at most 128 MiB of HBM per device.

```python
import math
import jax
import jax.numpy as jnp
from jax import lax

BLOCK = 128
K = 128
NCOL = 32768
RB_DEV = 16
BLK_CAP = 64
SLABS = 256
NCB = 256
BLOCKS = 16384
ROWS = 524288


def draw_block_rows(key, part):
    key = jax.random.fold_in(key, 11)
    extra = jax.random.randint(key, (SLABS, BLK_CAP), 0, RB_DEV)
    slots = jnp.arange(BLK_CAP, dtype=jnp.int32)
    local = jnp.where(slots[None, :] < RB_DEV, slots[None, :] % RB_DEV, extra)
    offsets = jnp.arange(SLABS, dtype=jnp.int32) * RB_DEV
    return (local + offsets[:, None]).reshape(BLOCKS).astype(jnp.int32)


def draw_block_cols(key, part):
    key = jax.random.fold_in(key, 23)
    return jax.random.randint(key, (BLOCKS,), 0, NCB).astype(jnp.int32)


def draw_block_count(key, part):
    key = jax.random.fold_in(key, 37)
    first_key, second_key = jax.random.split(key)
    counts = jax.random.randint(first_key, (SLABS,), RB_DEV, BLK_CAP + 1)
    fullest = jax.random.randint(second_key, (), 0, SLABS)
    counts = jnp.where(jnp.arange(SLABS, dtype=jnp.int32) == fullest, BLK_CAP, counts)
    return counts.astype(jnp.int32)


def steps_of(stream_key, dims, shards, smallest, top_value):
    gain, own = 1.0, jax.random.fold_in(stream_key, 6)
    for dim, blocks in shards:
        draws = jnp.exp(jax.random.uniform(jax.random.fold_in(own, dim), (blocks,), jnp.float32, smallest / len(shards), top_value / len(shards)))
        gain = gain * jnp.repeat(draws, dims[dim] // blocks).reshape([-1 if axis == dim else 1 for axis in range(len(dims))])
    return gain


def centred(stream_key, extent, width, most, cuts=(), kind=jnp.bfloat16):
    values = width * jax.random.normal(stream_key, extent, jnp.float32)
    if cuts:
        values = values * steps_of(stream_key, extent, cuts, -0.22, 0.18)
    return jnp.clip(values, -most, most).astype(kind)


def setup_inputs(seed: int = 0) -> dict:
    streams_of = jax.random.split(jax.random.key(seed), 6)
    block_values = centred(streams_of[0], (BLOCKS, BLOCK, BLOCK), 1.0, 6.0, ((0, 256),))
    block_rows = draw_block_rows(jax.random.fold_in(streams_of[5], 71), 0)
    block_cols = draw_block_cols(jax.random.fold_in(streams_of[5], 71), 0)
    block_count = draw_block_count(jax.random.fold_in(streams_of[5], 71), 0)
    test_matrix = centred(streams_of[4], (NCOL, K), (3 * BLOCK) ** -0.5, 0.3125, ((0, 256),))
    return dict(block_values=block_values, block_rows=block_rows, block_cols=block_cols, block_count=block_count, test_matrix=test_matrix)


def slab_sketch(values, row_ids, columns, live_count, omega_blocks):
    is_live = jnp.arange(BLK_CAP, dtype=jnp.int32) < live_count
    picked = omega_blocks[columns].astype(jnp.float32)
    products = jnp.einsum('sij,sjk->sik', values.astype(jnp.float32), picked)
    products = jnp.where(is_live[:, None, None], products, jnp.zeros_like(products))
    return jax.ops.segment_sum(products, row_ids, num_segments=RB_DEV)

def reference(block_values, block_rows, block_cols, block_count, test_matrix):
    values = block_values.reshape(SLABS, BLK_CAP, BLOCK, BLOCK)
    offsets = (jnp.arange(SLABS, dtype=jnp.int32) * RB_DEV).astype(jnp.int32)
    row_ids = (block_rows.reshape(SLABS, BLK_CAP) - offsets[:, None]).astype(jnp.int32)
    columns = block_cols.reshape(SLABS, BLK_CAP)
    omega_blocks = test_matrix.reshape(NCB, BLOCK, K)

    def one_slab(pieces):
        return slab_sketch(pieces[0], pieces[1], pieces[2], pieces[3], omega_blocks)
    sketch = lax.map(one_slab, (values, row_ids, columns, block_count)).reshape(ROWS, K)
    basis, upper = jnp.linalg.qr(sketch)
    signs = jnp.sign(jnp.diagonal(upper))
    basis = basis * signs[None, :]
    upper = upper * signs[:, None]
    q_basis = (basis * math.sqrt(ROWS)).astype(jnp.bfloat16)
    r_factor = upper / math.sqrt(ROWS)
    basis_slabs = q_basis.reshape(SLABS, RB_DEV, BLOCK, K)

    def add_slab(totals, pieces):
        slab_values, slab_rows, slab_cols, live_count, slab_basis = pieces
        is_live = jnp.arange(BLK_CAP, dtype=jnp.int32) < live_count
        picked = slab_basis[slab_rows].astype(jnp.float32)
        products = jnp.einsum('sji,sjk->sik', slab_values.astype(jnp.float32), picked)
        products = jnp.where(is_live[:, None, None], products, jnp.zeros_like(products))
        return (totals + jax.ops.segment_sum(products, slab_cols, num_segments=NCB), None)
    totals, _ = lax.scan(add_slab, jnp.zeros((NCB, BLOCK, K), jnp.float32), (values, row_ids, columns, block_count, basis_slabs))
    projected = totals.reshape(NCOL, K) * math.sqrt(NCOL / (BLOCKS * BLOCK))
    return (q_basis, r_factor, projected)
```

```python
import functools
import math

import jax
import jax.numpy as jnp
from jax import lax
from jax.experimental import pallas as pl
from jax.experimental.pallas import tpu as pltpu
from jax.sharding import PartitionSpec as P

NCOL = 32768
RB_DEV = 16
BLOCK = 128
HALF = 64
NX, NY, NZ = 4, 4, 8

MESH = pl.DeviceIdType.MESH
AXES = ("wide", "narrow")
VMEM_LIMIT = 52 * 1024 * 1024

precise = lax.Precision.HIGHEST


def place():
    wide = lax.axis_index("wide")
    narrow = lax.axis_index("narrow")
    return narrow // NY, narrow % NY, wide // 2, wide % 2


def at(x, y, z, core):
    return (z * 2 + core, x * NY + y)


def column_place(column):
    narrow = column % (NX * NY)
    wide = column // (NX * NY)
    return wide % 2, narrow // NY, narrow % NY, wide // 2


def loop(low, high, body):
    def step(index, carry):
        body(index)
        return carry

    lax.fori_loop(low, high, step, 0)


def greet_torus(x, y, z, core):
    barrier = pltpu.get_barrier_semaphore()

    def greet(device):
        pl.semaphore_signal(barrier, inc=1, device_id=device, device_id_type=MESH)

    loop(1, NX, lambda k: greet(at((x + k) % NX, y, z, core)))
    loop(1, NY, lambda k: greet(at(x, (y + k) % NY, z, core)))
    loop(1, NZ, lambda k: greet(at(x, y, (z + k) % NZ, core)))
    greet(at(x, y, z, 1 - core))
    pl.semaphore_wait(barrier, NX + NY + NZ - 2)


def remote(src, dst, send, recv, device):
    return pltpu.make_async_remote_copy(
        src_ref=src, dst_ref=dst, send_sem=send, recv_sem=recv, device_id=device, device_id_type=MESH
    )


def gather_kernel(mine, out, local_sem, sz, rz, sx, rx, sy, ry, sc, rc):
    x, y, z, core = place()
    other = 1 - core
    greet_torus(x, y, z, core)
    home = out.at[core, :, x, y, z]
    keep = pltpu.make_async_copy(mine, home, local_sem)
    keep.start()

    def along_z(k):
        return remote(mine, home, sz.at[k], rz.at[k], at(x, y, (z + k) % NZ, core))

    loop(1, NZ, lambda k: along_z(k).start())
    keep.wait()
    loop(1, NZ, lambda k: along_z(k).wait())

    def first_x(k):
        piece = out.at[core, 0, x, y]
        return remote(piece, piece, sx.at[0, k], rx.at[0, k], at((x + k) % NX, y, z, core))

    def first_y(k):
        piece = out.at[core, 1, x, y]
        return remote(piece, piece, sy.at[0, k], ry.at[0, k], at(x, (y + k) % NY, z, core))

    loop(1, NX, lambda k: first_x(k).start())
    loop(1, NY, lambda k: first_y(k).start())
    loop(1, NX, lambda k: first_x(k).wait())

    def second_y(k):
        piece = out.at[core, 0, :, y]
        return remote(piece, piece, sy.at[1, k], ry.at[1, k], at(x, (y + k) % NY, z, core))

    def second_x(k):
        piece = out.at[core, 1, x]
        return remote(piece, piece, sx.at[1, k], rx.at[1, k], at((x + k) % NX, y, z, core))

    def across_y(k):
        piece = out.at[core, 0, :, (y + NY - k) % NY]
        return remote(piece, piece, sc.at[0, k], rc.at[0, k], at(x, y, z, other))

    def across_x(k):
        piece = out.at[core, 1, (x + NX - k) % NX]
        return remote(piece, piece, sc.at[1, k], rc.at[1, k], at(x, y, z, other))

    loop(1, NY, lambda k: second_y(k).start())
    loop(1, NY, lambda k: first_y(k).wait())
    loop(1, NX, lambda k: second_x(k).start())
    across_y(0).start()
    across_x(0).start()

    def pass_y(k):
        second_y(k).wait_recv()
        across_y(k).start()

    def pass_x(k):
        second_x(k).wait_recv()
        across_x(k).start()

    loop(1, NY, pass_y)
    loop(1, NX, pass_x)
    loop(1, NY, lambda k: second_y(k).wait_send())
    loop(1, NX, lambda k: second_x(k).wait_send())
    loop(0, NY, lambda k: across_y(k).wait())
    loop(0, NX, lambda k: across_x(k).wait())


def gather_rows(test_matrix):
    width = test_matrix.shape[1]
    dma = pltpu.SemaphoreType.DMA
    return pl.pallas_call(
        gather_kernel,
        out_shape=jax.ShapeDtypeStruct((2, 2, NX, NY, NZ, HALF, width), jnp.bfloat16),
        in_specs=[pl.BlockSpec(memory_space=pl.ANY)],
        out_specs=pl.BlockSpec(memory_space=pl.ANY),
        scratch_shapes=[
            dma,
            dma((NZ,)),
            dma((NZ,)),
            dma((2, NX)),
            dma((2, NX)),
            dma((2, NY)),
            dma((2, NY)),
            dma((2, max(NX, NY))),
            dma((2, max(NX, NY))),
        ],
        compiler_params=pltpu.CompilerParams(collective_id=0, has_side_effects=True),
        name="gather_rows",
    )(test_matrix.reshape(2, HALF, width))


def total_kernel(part, out, got, mid, got_wide, s1, r1, s2, r2, s3, r3):
    wide = lax.axis_index("wide")
    narrow = lax.axis_index("narrow")
    wides, narrows = 2 * NZ, NX * NY
    rows = part.shape[0] // narrows

    barrier = pltpu.get_barrier_semaphore()

    def greet(device):
        pl.semaphore_signal(barrier, inc=1, device_id=device, device_id_type=MESH)

    loop(1, narrows, lambda k: greet((wide, (narrow + k) % narrows)))
    loop(1, wides, lambda k: greet(((wide + k) % wides, narrow)))
    pl.semaphore_wait(barrier, narrows + wides - 2)

    def chunk(ref, index):
        return ref.at[pl.ds(pl.multiple_of(index * rows, rows), rows)]

    def scatter(k):
        peer = (narrow + k) % narrows
        return remote(chunk(part, peer), got.at[narrow], s1.at[k], r1.at[k], (wide, peer))

    loop(1, narrows, lambda k: scatter(k).start())
    got[narrow] = chunk(part, narrow)[...]
    loop(1, narrows, lambda k: scatter(k).wait())
    total = got[0]
    for index in range(1, narrows):
        total = total + got[index]
    mid[...] = total

    def exchange(k):
        return remote(mid, got_wide.at[wide], s2.at[k], r2.at[k], ((wide + k) % wides, narrow))

    loop(1, wides, lambda k: exchange(k).start())
    got_wide[wide] = total
    loop(1, wides, lambda k: exchange(k).wait())
    total = got_wide[0]
    for index in range(1, wides):
        total = total + got_wide[index]
    chunk(out, narrow)[...] = total

    def spread(k):
        piece = chunk(out, narrow)
        return remote(piece, piece, s3.at[k], r3.at[k], (wide, (narrow + k) % narrows))

    loop(1, narrows, lambda k: spread(k).start())
    loop(1, narrows, lambda k: spread(k).wait())


def total_over_devices(matrix, collective_id):
    narrows, wides = NX * NY, 2 * NZ
    rows, width = matrix.shape[0] // narrows, matrix.shape[1]
    dma = pltpu.SemaphoreType.DMA
    return pl.pallas_call(
        total_kernel,
        out_shape=jax.ShapeDtypeStruct(matrix.shape, jnp.float32),
        in_specs=[pl.BlockSpec(memory_space=pltpu.VMEM)],
        out_specs=pl.BlockSpec(memory_space=pltpu.VMEM),
        scratch_shapes=[
            pltpu.VMEM((narrows, rows, width), jnp.float32),
            pltpu.VMEM((rows, width), jnp.float32),
            pltpu.VMEM((wides, rows, width), jnp.float32),
            dma((narrows,)),
            dma((narrows,)),
            dma((wides,)),
            dma((wides,)),
            dma((narrows,)),
            dma((narrows,)),
        ],
        compiler_params=pltpu.CompilerParams(collective_id=collective_id, has_side_effects=True),
        name="total_gram",
    )(matrix)


def scatter_kernel(
    scale, share, out, own, got, part0, part1, last, a0, a1, b0, b1, cz, so, sc, rc, sa, ra, sb, rb, sz, rz
):
    x, y, z, core = place()
    other = 1 - core
    f32, bf16 = jnp.float32, jnp.bfloat16

    def mine0(k):
        to = (x + k) % NX
        return pltpu.make_async_copy(share.at[core, 0, to], own.at[0, to], so.at[0, k])

    def mine1(k):
        to = (y + k) % NY
        return pltpu.make_async_copy(share.at[core, 1, :, to], own.at[1, :, to], so.at[1, k])

    def across0(k):
        to = (x + k) % NX
        return remote(share.at[other, 0, to], got.at[0, to], sc.at[0, k], rc.at[0, k], at(x, y, z, other))

    def across1(k):
        to = (y + k) % NY
        return remote(share.at[other, 1, :, to], got.at[1, :, to], sc.at[1, k], rc.at[1, k], at(x, y, z, other))

    def first0(k):
        device = at((x + k) % NX, y, z, core)
        return remote(own.at[0, (x + k) % NX], a0.at[k - 1], sa.at[0, k], ra.at[0, k], device)

    def first1(k):
        device = at(x, (y + k) % NY, z, core)
        return remote(own.at[1, :, (y + k) % NY], a1.at[k - 1], sa.at[1, k], ra.at[1, k], device)

    def second0(k):
        device = at(x, (y + k) % NY, z, core)
        return remote(part0.at[(y + k) % NY], b0.at[k - 1], sb.at[0, k], rb.at[0, k], device)

    def second1(k):
        device = at((x + k) % NX, y, z, core)
        return remote(part1.at[(x + k) % NX], b1.at[k - 1], sb.at[1, k], rb.at[1, k], device)

    def third(k):
        device = at(x, y, (z + k) % NZ, core)
        return remote(last.at[(z + k) % NZ], cz.at[k - 1], sz.at[k], rz.at[k], device)

    loop(0, NX, lambda k: mine0(k).start())
    loop(0, NY, lambda k: mine1(k).start())
    greet_torus(x, y, z, core)
    for k in [*range(1, max(NX, NY)), 0]:
        if k < NX:
            across0(k).start()
        if k < NY:
            across1(k).start()

    def join0(k):
        to = (x + k) % NX
        mine0(k).wait()
        across0(k).wait_recv()

        def add(i):
            own[0, to, i] = (own[0, to, i].astype(f32) + got[0, to, i].astype(f32)).astype(bf16)

        loop(0, NY, add)

    def join1(k):
        to = (y + k) % NY
        mine1(k).wait()
        across1(k).wait_recv()

        def add(i):
            own[1, i, to] = (own[1, i, to].astype(f32) + got[1, i, to].astype(f32)).astype(bf16)

        loop(0, NX, add)

    for k in range(1, max(NX, NY)):
        if k < NX:
            join0(k)
            first0(k).start()
        if k < NY:
            join1(k)
            first1(k).start()
    join0(0)
    join1(0)

    loop(1, NX, lambda k: first0(k).wait_recv())

    def sum0(i):
        total = own[0, x, i].astype(f32)
        for k in range(NX - 1):
            total = total + a0[k, i].astype(f32)
        part0[i] = total.astype(bf16)

    loop(0, NY, sum0)
    loop(1, NY, lambda k: second0(k).start())
    loop(1, NY, lambda k: first1(k).wait_recv())

    def sum1(i):
        total = own[1, i, y].astype(f32)
        for k in range(NY - 1):
            total = total + a1[k, i].astype(f32)
        part1[i] = total.astype(bf16)

    loop(0, NX, sum1)
    loop(1, NX, lambda k: second1(k).start())
    loop(1, NY, lambda k: second0(k).wait_recv())
    loop(1, NX, lambda k: second1(k).wait_recv())

    def sum_last(i):
        total = part0[y, i].astype(f32)
        for k in range(NY - 1):
            total = total + b0[k, i].astype(f32)
        last[i, 0] = total.astype(bf16)
        total = part1[x, i].astype(f32)
        for k in range(NX - 1):
            total = total + b1[k, i].astype(f32)
        last[i, 1] = total.astype(bf16)

    loop(0, NZ, sum_last)
    loop(1, NZ, lambda k: third(k).start())
    loop(1, NZ, lambda k: third(k).wait_recv())
    total = last[z].astype(f32)
    for k in range(NZ - 1):
        total = total + cz[k].astype(f32)
    out[...] = total * scale

    loop(0, NX, lambda k: across0(k).wait_send())
    loop(0, NY, lambda k: across1(k).wait_send())
    loop(1, NX, lambda k: first0(k).wait_send())
    loop(1, NY, lambda k: first1(k).wait_send())
    loop(1, NY, lambda k: second0(k).wait_send())
    loop(1, NX, lambda k: second1(k).wait_send())
    loop(1, NZ, lambda k: third(k).wait_send())


def scatter_shares(share, scale):
    width = share.shape[-1]
    bf16 = jnp.bfloat16
    dma = pltpu.SemaphoreType.DMA
    longer = max(NX, NY)
    tail = (NZ, HALF, width)
    vmem = pltpu.VMEM
    summed = pl.pallas_call(
        functools.partial(scatter_kernel, scale),
        out_shape=jax.ShapeDtypeStruct((2, HALF, width), jnp.float32),
        in_specs=[pl.BlockSpec(memory_space=pl.ANY)],
        out_specs=pl.BlockSpec(memory_space=pltpu.VMEM),
        scratch_shapes=[
            vmem((2, NX, NY, *tail), bf16),
            vmem((2, NX, NY, *tail), bf16),
            vmem((NY, *tail), bf16),
            vmem((NX, *tail), bf16),
            vmem((NZ, 2, HALF, width), bf16),
            vmem((NX - 1, NY, *tail), bf16),
            vmem((NY - 1, NX, *tail), bf16),
            vmem((NY - 1, *tail), bf16),
            vmem((NX - 1, *tail), bf16),
            vmem((NZ - 1, 2, HALF, width), bf16),
            dma((2, longer)),
            dma((2, longer)),
            dma((2, longer)),
            dma((2, longer)),
            dma((2, longer)),
            dma((2, longer)),
            dma((2, longer)),
            dma((NZ,)),
            dma((NZ,)),
        ],
        compiler_params=pltpu.CompilerParams(
            collective_id=3, has_side_effects=True, vmem_limit_bytes=VMEM_LIMIT
        ),
        name="scatter_shares",
    )(share)
    return summed.reshape(2 * HALF, width)


UNROLL = 4


def sketch_kernel(columns, rows, count, values, omega, out):
    out[...] = jnp.zeros_like(out)
    live = count[0]

    def some(step):
        for u in range(UNROLL):
            slot = step * UNROLL + u
            core, x, y, z = column_place(columns[slot])
            picked = jnp.concatenate([omega[core, 0, x, y, z], omega[core, 1, x, y, z]], axis=0)
            product = jnp.dot(values[slot], picked, preferred_element_type=jnp.float32)
            row = rows[slot]
            out[row] = out[row] + jnp.where(slot < live, product, 0.0)

    loop(0, (live + UNROLL - 1) // UNROLL, some)


def sketch_slab(values, columns, rows, count, omega):
    width = omega.shape[-1]
    smem = pl.BlockSpec(memory_space=pltpu.SMEM)
    vmem = pl.BlockSpec(memory_space=pltpu.VMEM)
    return pl.pallas_call(
        sketch_kernel,
        out_shape=jax.ShapeDtypeStruct((RB_DEV, BLOCK, width), jnp.float32),
        in_specs=[smem, smem, smem, vmem, vmem],
        out_specs=vmem,
        compiler_params=pltpu.CompilerParams(vmem_limit_bytes=VMEM_LIMIT),
        name="sketch_slab",
    )(columns, rows, count, values, omega)


def project_kernel(columns, rows, count, values, basis, out, total):
    live = count[0]

    def clear(step):
        for core in range(2):
            for half in range(2):
                total[core, half, step // NY, step % NY] = jnp.zeros(total.shape[4:], jnp.float32)

    loop(0, NX * NY, clear)

    def some(step):
        for u in range(UNROLL):
            slot = step * UNROLL + u
            core, x, y, z = column_place(columns[slot])
            product = lax.dot_general(
                values[slot], basis[rows[slot]], (((0,), (0,)), ((), ())), preferred_element_type=jnp.float32
            )
            product = jnp.where(slot < live, product, 0.0)
            total[core, 0, x, y, z] = total[core, 0, x, y, z] + product[:HALF]
            total[core, 1, x, y, z] = total[core, 1, x, y, z] + product[HALF:]

    loop(0, (live + UNROLL - 1) // UNROLL, some)

    def narrow(step):
        x, y = step // NY, step % NY
        for core in range(2):
            for half in range(2):
                out[core, half, x, y] = total[core, half, x, y].astype(jnp.bfloat16)

    loop(0, NX * NY, narrow)


def project_slab(values, columns, rows, count, basis):
    width = basis.shape[-1]
    smem = pl.BlockSpec(memory_space=pltpu.SMEM)
    vmem = pl.BlockSpec(memory_space=pltpu.VMEM)
    shape = (2, 2, NX, NY, NZ, HALF, width)
    return pl.pallas_call(
        project_kernel,
        out_shape=jax.ShapeDtypeStruct(shape, jnp.bfloat16),
        in_specs=[smem, smem, smem, vmem, vmem],
        out_specs=vmem,
        scratch_shapes=[pltpu.VMEM(shape, jnp.float32)],
        compiler_params=pltpu.CompilerParams(vmem_limit_bytes=VMEM_LIMIT),
        name="project_slab",
    )(columns, rows, count, values, basis)


def factor_lower(row_block, collective_id):
    gram_matrix = jnp.dot(
        row_block.T, row_block, precision=precise, preferred_element_type=jnp.float32
    )
    return jnp.linalg.cholesky(total_over_devices(gram_matrix, collective_id))


def right_divide(row_block, lower_part):
    return lax.linalg.triangular_solve(
        lower_part, row_block, left_side=False, lower=True, transpose_a=True
    )


def on_device(block_values, block_rows, block_cols, block_count, test_matrix):
    slot_count, width_block, _ = block_values.shape
    sketch_width = test_matrix.shape[1]
    slab_total = lax.axis_size("wide") * lax.axis_size("narrow")
    slab_index = lax.axis_index(AXES)
    local_rows = block_rows - slab_index * RB_DEV
    omega = gather_rows(test_matrix)
    sketch = sketch_slab(block_values, block_cols, local_rows, block_count, omega)
    sketch = sketch.reshape(RB_DEV * width_block, sketch_width)
    lower_one = factor_lower(sketch, 1)
    first_basis = right_divide(sketch, lower_one)
    lower_two = factor_lower(first_basis, 2)
    second_basis = right_divide(first_basis, lower_two)
    total_rows = sketch.shape[0] * slab_total
    q_basis = (second_basis * math.sqrt(total_rows)).astype(jnp.bfloat16)
    r_factor = jnp.dot(
        lower_one, lower_two, precision=precise, preferred_element_type=jnp.float32
    ).T / math.sqrt(total_rows)
    basis_blocks = q_basis.reshape(RB_DEV, width_block, sketch_width)
    share = project_slab(block_values, block_cols, local_rows, block_count, basis_blocks)
    column_scale = math.sqrt(NCOL / (slot_count * slab_total * width_block))
    projected = scatter_shares(share, column_scale)
    return (q_basis, r_factor, projected)


def solution(mesh):
    placed = (
        P(AXES, None, None),
        P(AXES),
        P(AXES),
        P(AXES),
        P(AXES, None),
    )
    return jax.shard_map(
        on_device,
        mesh=mesh,
        in_specs=placed,
        out_specs=(P(AXES, None), P(), P(AXES, None)),
        check_vma=False,
    )
```

```python
import math

import jax
import jax.numpy as jnp
from jax import lax
from jax.experimental import pallas as pl
from jax.experimental.pallas import tpu as pltpu
from jax.sharding import PartitionSpec as P

NCOL = 32768
RB_DEV = 16
BLOCK = 128
HALF = 64
NX, NY, NZ = 4, 4, 8

MESH = pl.DeviceIdType.MESH
AXES = ("wide", "narrow")
VMEM_LIMIT = 52 * 1024 * 1024

precise = lax.Precision.HIGHEST


def place():
    wide = lax.axis_index("wide")
    narrow = lax.axis_index("narrow")
    return narrow // NY, narrow % NY, wide // 2, wide % 2


def at(x, y, z, core):
    return (z * 2 + core, x * NY + y)


def column_place(column):
    narrow = column % (NX * NY)
    wide = column // (NX * NY)
    return wide % 2, narrow // NY, narrow % NY, wide // 2


def loop(low, high, body):
    def step(index, carry):
        body(index)
        return carry

    lax.fori_loop(low, high, step, 0)


def greet_torus(x, y, z, core):
    barrier = pltpu.get_barrier_semaphore()

    def greet(device):
        pl.semaphore_signal(barrier, inc=1, device_id=device, device_id_type=MESH)

    loop(1, NX, lambda k: greet(at((x + k) % NX, y, z, core)))
    loop(1, NY, lambda k: greet(at(x, (y + k) % NY, z, core)))
    loop(1, NZ, lambda k: greet(at(x, y, (z + k) % NZ, core)))
    greet(at(x, y, z, 1 - core))
    pl.semaphore_wait(barrier, NX + NY + NZ - 2)


def remote(src, dst, send, recv, device):
    return pltpu.make_async_remote_copy(
        src_ref=src, dst_ref=dst, send_sem=send, recv_sem=recv, device_id=device, device_id_type=MESH
    )


def gather_kernel(mine, out, local_sem, sz, rz, sx, rx, sy, ry, sc, rc):
    x, y, z, core = place()
    other = 1 - core
    greet_torus(x, y, z, core)
    home = out.at[core, :, x, y, z]
    keep = pltpu.make_async_copy(mine, home, local_sem)
    keep.start()

    def along_z(k):
        return remote(mine, home, sz.at[k], rz.at[k], at(x, y, (z + k) % NZ, core))

    loop(1, NZ, lambda k: along_z(k).start())
    keep.wait()
    loop(1, NZ, lambda k: along_z(k).wait())

    def first_x(k):
        piece = out.at[core, 0, x, y]
        return remote(piece, piece, sx.at[0, k], rx.at[0, k], at((x + k) % NX, y, z, core))

    def first_y(k):
        piece = out.at[core, 1, x, y]
        return remote(piece, piece, sy.at[0, k], ry.at[0, k], at(x, (y + k) % NY, z, core))

    loop(1, NX, lambda k: first_x(k).start())
    loop(1, NY, lambda k: first_y(k).start())
    loop(1, NX, lambda k: first_x(k).wait())

    def second_y(k):
        piece = out.at[core, 0, :, y]
        return remote(piece, piece, sy.at[1, k], ry.at[1, k], at(x, (y + k) % NY, z, core))

    def second_x(k):
        piece = out.at[core, 1, x]
        return remote(piece, piece, sx.at[1, k], rx.at[1, k], at((x + k) % NX, y, z, core))

    def across_y(k):
        piece = out.at[core, 0, :, (y + NY - k) % NY]
        return remote(piece, piece, sc.at[0, k], rc.at[0, k], at(x, y, z, other))

    def across_x(k):
        piece = out.at[core, 1, (x + NX - k) % NX]
        return remote(piece, piece, sc.at[1, k], rc.at[1, k], at(x, y, z, other))

    loop(1, NY, lambda k: second_y(k).start())
    loop(1, NY, lambda k: first_y(k).wait())
    loop(1, NX, lambda k: second_x(k).start())
    across_y(0).start()
    across_x(0).start()

    def pass_y(k):
        second_y(k).wait_recv()
        across_y(k).start()

    def pass_x(k):
        second_x(k).wait_recv()
        across_x(k).start()

    loop(1, NY, pass_y)
    loop(1, NX, pass_x)
    loop(1, NY, lambda k: second_y(k).wait_send())
    loop(1, NX, lambda k: second_x(k).wait_send())
    loop(0, NY, lambda k: across_y(k).wait())
    loop(0, NX, lambda k: across_x(k).wait())


def gather_rows(test_matrix):
    width = test_matrix.shape[1]
    dma = pltpu.SemaphoreType.DMA
    return pl.pallas_call(
        gather_kernel,
        out_shape=jax.ShapeDtypeStruct((2, 2, NX, NY, NZ, HALF, width), jnp.bfloat16),
        in_specs=[pl.BlockSpec(memory_space=pl.ANY)],
        out_specs=pl.BlockSpec(memory_space=pl.ANY),
        scratch_shapes=[
            dma,
            dma((NZ,)),
            dma((NZ,)),
            dma((2, NX)),
            dma((2, NX)),
            dma((2, NY)),
            dma((2, NY)),
            dma((2, max(NX, NY))),
            dma((2, max(NX, NY))),
        ],
        compiler_params=pltpu.CompilerParams(collective_id=0, has_side_effects=True),
        name="gather_rows",
    )(test_matrix.reshape(2, HALF, width))


class gram_steps:
    def __init__(self, part, out, got, mid, got_wide, s1, r1, s2, r2, s3, r3):
        self.part, self.out, self.got, self.mid, self.got_wide = part, out, got, mid, got_wide
        self.s1, self.r1, self.s2, self.r2, self.s3, self.r3 = s1, r1, s2, r2, s3, r3
        self.wide, self.narrow = lax.axis_index("wide"), lax.axis_index("narrow")
        self.wides, self.narrows = 2 * NZ, NX * NY
        self.rows = part.shape[0] // self.narrows

    def greet(self):
        wide, narrow, wides, narrows = self.wide, self.narrow, self.wides, self.narrows
        barrier = pltpu.get_barrier_semaphore()

        def one(device):
            pl.semaphore_signal(barrier, inc=1, device_id=device, device_id_type=MESH)

        loop(1, narrows, lambda k: one((wide, (narrow + k) % narrows)))
        loop(1, wides, lambda k: one(((wide + k) % wides, narrow)))
        pl.semaphore_wait(barrier, narrows + wides - 2)

    def chunk(self, ref, index):
        return ref.at[pl.ds(pl.multiple_of(index * self.rows, self.rows), self.rows)]

    def scatter(self, k):
        peer = (self.narrow + k) % self.narrows
        source = self.chunk(self.part, peer)
        return remote(source, self.got.at[self.narrow], self.s1.at[k], self.r1.at[k], (self.wide, peer))

    def exchange(self, k):
        device = ((self.wide + k) % self.wides, self.narrow)
        return remote(self.mid, self.got_wide.at[self.wide], self.s2.at[k], self.r2.at[k], device)

    def spread(self, k):
        piece = self.chunk(self.out, self.narrow)
        device = (self.wide, (self.narrow + k) % self.narrows)
        return remote(piece, piece, self.s3.at[k], self.r3.at[k], device)

    def scatter_start(self):
        loop(1, self.narrows, lambda k: self.scatter(k).start())
        self.got[self.narrow] = self.chunk(self.part, self.narrow)[...]

    def scatter_finish(self):
        loop(1, self.narrows, lambda k: self.scatter(k).wait())
        total = self.got[0]
        for index in range(1, self.narrows):
            total = total + self.got[index]
        self.mid[...] = total
        self.got_wide[self.wide] = total
        loop(1, self.wides, lambda k: self.exchange(k).start())

    def exchange_finish(self):
        loop(1, self.wides, lambda k: self.exchange(k).wait())
        total = self.got_wide[0]
        for index in range(1, self.wides):
            total = total + self.got_wide[index]
        self.chunk(self.out, self.narrow)[...] = total
        loop(1, self.narrows, lambda k: self.spread(k).start())

    def spread_finish(self):
        loop(1, self.narrows, lambda k: self.spread(k).wait())


def total_kernel(part, out, got, mid, got_wide, s1, r1, s2, r2, s3, r3):
    gram = gram_steps(part, out, got, mid, got_wide, s1, r1, s2, r2, s3, r3)
    gram.greet()
    gram.scatter_start()
    gram.scatter_finish()
    gram.exchange_finish()
    gram.spread_finish()


def total_over_devices(matrix, collective_id):
    narrows, wides = NX * NY, 2 * NZ
    rows, width = matrix.shape[0] // narrows, matrix.shape[1]
    dma = pltpu.SemaphoreType.DMA
    return pl.pallas_call(
        total_kernel,
        out_shape=jax.ShapeDtypeStruct(matrix.shape, jnp.float32),
        in_specs=[pl.BlockSpec(memory_space=pltpu.VMEM)],
        out_specs=pl.BlockSpec(memory_space=pltpu.VMEM),
        scratch_shapes=[
            pltpu.VMEM((narrows, rows, width), jnp.float32),
            pltpu.VMEM((rows, width), jnp.float32),
            pltpu.VMEM((wides, rows, width), jnp.float32),
            dma((narrows,)),
            dma((narrows,)),
            dma((wides,)),
            dma((wides,)),
            dma((narrows,)),
            dma((narrows,)),
        ],
        compiler_params=pltpu.CompilerParams(collective_id=collective_id, has_side_effects=True),
        name="total_gram",
    )(matrix)


def scatter_kernel(
    share, part, out, whole, own, got, part0, part1, last, a0, a1, b0, b1, cz, got_narrow, mid, got_wide,
    so, sc, rc, sa, ra, sb, rb, sz, rz, s1, r1, s2, r2, s3, r3,
):
    x, y, z, core = place()
    gram = gram_steps(part, whole, got_narrow, mid, got_wide, s1, r1, s2, r2, s3, r3)
    other = 1 - core
    f32, bf16 = jnp.float32, jnp.bfloat16

    def mine0(k):
        to = (x + k) % NX
        return pltpu.make_async_copy(share.at[core, 0, to], own.at[0, to], so.at[0, k])

    def mine1(k):
        to = (y + k) % NY
        return pltpu.make_async_copy(share.at[core, 1, :, to], own.at[1, :, to], so.at[1, k])

    def across0(k):
        to = (x + k) % NX
        return remote(share.at[other, 0, to], got.at[0, to], sc.at[0, k], rc.at[0, k], at(x, y, z, other))

    def across1(k):
        to = (y + k) % NY
        return remote(share.at[other, 1, :, to], got.at[1, :, to], sc.at[1, k], rc.at[1, k], at(x, y, z, other))

    def first0(k):
        device = at((x + k) % NX, y, z, core)
        return remote(own.at[0, (x + k) % NX], a0.at[k - 1], sa.at[0, k], ra.at[0, k], device)

    def first1(k):
        device = at(x, (y + k) % NY, z, core)
        return remote(own.at[1, :, (y + k) % NY], a1.at[k - 1], sa.at[1, k], ra.at[1, k], device)

    def second0(k):
        device = at(x, (y + k) % NY, z, core)
        return remote(part0.at[(y + k) % NY], b0.at[k - 1], sb.at[0, k], rb.at[0, k], device)

    def second1(k):
        device = at((x + k) % NX, y, z, core)
        return remote(part1.at[(x + k) % NX], b1.at[k - 1], sb.at[1, k], rb.at[1, k], device)

    def third(k):
        device = at(x, y, (z + k) % NZ, core)
        return remote(last.at[(z + k) % NZ], cz.at[k - 1], sz.at[k], rz.at[k], device)

    loop(0, NX, lambda k: mine0(k).start())
    loop(0, NY, lambda k: mine1(k).start())
    gram.greet()
    gram.scatter_start()
    for k in [*range(1, max(NX, NY)), 0]:
        if k < NX:
            across0(k).start()
        if k < NY:
            across1(k).start()

    def join0(k):
        to = (x + k) % NX
        mine0(k).wait()
        across0(k).wait_recv()

        def add(i):
            own[0, to, i] = (own[0, to, i].astype(f32) + got[0, to, i].astype(f32)).astype(bf16)

        loop(0, NY, add)

    def join1(k):
        to = (y + k) % NY
        mine1(k).wait()
        across1(k).wait_recv()

        def add(i):
            own[1, i, to] = (own[1, i, to].astype(f32) + got[1, i, to].astype(f32)).astype(bf16)

        loop(0, NX, add)

    for k in range(1, max(NX, NY)):
        if k < NX:
            join0(k)
            first0(k).start()
        if k < NY:
            join1(k)
            first1(k).start()
    gram.scatter_finish()
    join0(0)
    join1(0)
    gram.exchange_finish()

    loop(1, NX, lambda k: first0(k).wait_recv())

    def sum0(i):
        total = own[0, x, i].astype(f32)
        for k in range(NX - 1):
            total = total + a0[k, i].astype(f32)
        part0[i] = total.astype(bf16)

    loop(0, NY, sum0)
    loop(1, NY, lambda k: second0(k).start())
    loop(1, NY, lambda k: first1(k).wait_recv())

    def sum1(i):
        total = own[1, i, y].astype(f32)
        for k in range(NY - 1):
            total = total + a1[k, i].astype(f32)
        part1[i] = total.astype(bf16)

    loop(0, NX, sum1)
    loop(1, NX, lambda k: second1(k).start())
    loop(1, NY, lambda k: second0(k).wait_recv())
    loop(1, NX, lambda k: second1(k).wait_recv())

    def sum_last(i):
        total = part0[y, i].astype(f32)
        for k in range(NY - 1):
            total = total + b0[k, i].astype(f32)
        last[i, 0] = total.astype(bf16)
        total = part1[x, i].astype(f32)
        for k in range(NX - 1):
            total = total + b1[k, i].astype(f32)
        last[i, 1] = total.astype(bf16)

    loop(0, NZ, sum_last)
    loop(1, NZ, lambda k: third(k).start())
    loop(1, NZ, lambda k: third(k).wait_recv())
    total = last[z].astype(f32)
    for k in range(NZ - 1):
        total = total + cz[k].astype(f32)
    out[...] = total

    gram.spread_finish()
    loop(0, NX, lambda k: across0(k).wait_send())
    loop(0, NY, lambda k: across1(k).wait_send())
    loop(1, NX, lambda k: first0(k).wait_send())
    loop(1, NY, lambda k: first1(k).wait_send())
    loop(1, NY, lambda k: second0(k).wait_send())
    loop(1, NX, lambda k: second1(k).wait_send())
    loop(1, NZ, lambda k: third(k).wait_send())


def scatter_shares(share, gram, collective_id):
    width = share.shape[-1]
    bf16 = jnp.bfloat16
    dma = pltpu.SemaphoreType.DMA
    longer = max(NX, NY)
    tail = (NZ, HALF, width)
    vmem = pltpu.VMEM
    narrows, wides = NX * NY, 2 * NZ
    rows = gram.shape[0] // narrows
    in_vmem = pl.BlockSpec(memory_space=pltpu.VMEM)
    summed, whole = pl.pallas_call(
        scatter_kernel,
        out_shape=(
            jax.ShapeDtypeStruct((2, HALF, width), jnp.float32),
            jax.ShapeDtypeStruct(gram.shape, jnp.float32),
        ),
        in_specs=[pl.BlockSpec(memory_space=pl.ANY), in_vmem],
        out_specs=(in_vmem, in_vmem),
        scratch_shapes=[
            vmem((2, NX, NY, *tail), bf16),
            vmem((2, NX, NY, *tail), bf16),
            vmem((NY, *tail), bf16),
            vmem((NX, *tail), bf16),
            vmem((NZ, 2, HALF, width), bf16),
            vmem((NX - 1, NY, *tail), bf16),
            vmem((NY - 1, NX, *tail), bf16),
            vmem((NY - 1, *tail), bf16),
            vmem((NX - 1, *tail), bf16),
            vmem((NZ - 1, 2, HALF, width), bf16),
            vmem((narrows, rows, width), jnp.float32),
            vmem((rows, width), jnp.float32),
            vmem((wides, rows, width), jnp.float32),
            dma((2, longer)),
            dma((2, longer)),
            dma((2, longer)),
            dma((2, longer)),
            dma((2, longer)),
            dma((2, longer)),
            dma((2, longer)),
            dma((NZ,)),
            dma((NZ,)),
            dma((narrows,)),
            dma((narrows,)),
            dma((wides,)),
            dma((wides,)),
            dma((narrows,)),
            dma((narrows,)),
        ],
        compiler_params=pltpu.CompilerParams(
            collective_id=collective_id, has_side_effects=True, vmem_limit_bytes=VMEM_LIMIT
        ),
        name="scatter_shares",
    )(share, gram)
    return summed.reshape(2 * HALF, width), whole


UNROLL = 4


def slab_kernel(columns, rows, count, values_hbm, omega_hbm, sketch, gram, share, values, omega, total, packed, rounded, sv, so, sw):
    live = count[0]
    steps = (live + UNROLL - 1) // UNROLL
    bring_values = pltpu.make_async_copy(values_hbm, values, sv)
    bring_omega = pltpu.make_async_copy(omega_hbm, omega, so)
    bring_values.start()
    bring_omega.start()
    sketch[...] = jnp.zeros_like(sketch)

    def clear(step):
        for core in range(2):
            for half in range(2):
                total[core, half, step // NY, step % NY] = jnp.zeros(total.shape[4:], jnp.float32)

    loop(0, NX * NY, clear)
    bring_values.wait()
    bring_omega.wait()

    def add_sketch(step):
        for u in range(UNROLL):
            slot = step * UNROLL + u
            core, x, y, z = column_place(columns[slot])
            picked = jnp.concatenate([omega[core, 0, x, y, z], omega[core, 1, x, y, z]], axis=0)
            product = jnp.dot(values[slot], picked, preferred_element_type=jnp.float32)
            row = rows[slot]
            sketch[row] = sketch[row] + jnp.where(slot < live, product, 0.0)

    loop(0, steps, add_sketch)
    gram[...] = jnp.zeros_like(gram)

    def add_gram(step):
        for u in range(UNROLL):
            part = sketch[step * UNROLL + u]
            rounded[step * UNROLL + u] = part.astype(jnp.bfloat16)
            gram[...] += lax.dot_general(
                part, part, (((0,), (0,)), ((), ())), precision=precise, preferred_element_type=jnp.float32
            )

    loop(0, sketch.shape[0] // UNROLL, add_gram)

    def add_share(step):
        for u in range(UNROLL):
            slot = step * UNROLL + u
            core, x, y, z = column_place(columns[slot])
            product = lax.dot_general(
                values[slot], rounded[rows[slot]], (((0,), (0,)), ((), ())), preferred_element_type=jnp.float32
            )
            product = jnp.where(slot < live, product, 0.0)
            total[core, 0, x, y, z] = total[core, 0, x, y, z] + product[:HALF]
            total[core, 1, x, y, z] = total[core, 1, x, y, z] + product[HALF:]

    loop(0, steps, add_share)

    def hand_out(core, half, x):
        return pltpu.make_async_copy(packed.at[core, half, x], share.at[core, half, x], sw.at[core, half, x])

    def pack(x):
        for core in range(2):
            for half in range(2):

                def one(y):
                    packed[core, half, x, y] = total[core, half, x, y].astype(jnp.bfloat16)

                loop(0, NY, one)
                hand_out(core, half, x).start()

    loop(0, NX, pack)

    def done(x):
        for core in range(2):
            for half in range(2):
                hand_out(core, half, x).wait()

    loop(0, NX, done)


def slab_products(values, columns, rows, count, omega):
    width = omega.shape[-1]
    smem = pl.BlockSpec(memory_space=pltpu.SMEM)
    vmem = pl.BlockSpec(memory_space=pltpu.VMEM)
    hbm = pl.BlockSpec(memory_space=pl.ANY)
    dma = pltpu.SemaphoreType.DMA
    f32, bf16 = jnp.float32, jnp.bfloat16
    return pl.pallas_call(
        slab_kernel,
        out_shape=(
            jax.ShapeDtypeStruct((RB_DEV, BLOCK, width), f32),
            jax.ShapeDtypeStruct((width, width), f32),
            jax.ShapeDtypeStruct(omega.shape, bf16),
        ),
        in_specs=[smem, smem, smem, hbm, hbm],
        out_specs=(vmem, vmem, hbm),
        scratch_shapes=[
            pltpu.VMEM(values.shape, bf16),
            pltpu.VMEM(omega.shape, bf16),
            pltpu.VMEM(omega.shape, f32),
            pltpu.VMEM(omega.shape, bf16),
            pltpu.VMEM((RB_DEV, BLOCK, width), bf16),
            dma,
            dma,
            dma((2, 2, NX)),
        ],
        compiler_params=pltpu.CompilerParams(vmem_limit_bytes=VMEM_LIMIT),
        name="slab_products",
    )(columns, rows, count, values, omega)


def project_kernel(columns, rows, count, values, basis, out, total):
    live = count[0]

    def clear(step):
        for core in range(2):
            for half in range(2):
                total[core, half, step // NY, step % NY] = jnp.zeros(total.shape[4:], jnp.float32)

    loop(0, NX * NY, clear)

    def some(step):
        for u in range(UNROLL):
            slot = step * UNROLL + u
            core, x, y, z = column_place(columns[slot])
            product = lax.dot_general(
                values[slot], basis[rows[slot]], (((0,), (0,)), ((), ())), preferred_element_type=jnp.float32
            )
            product = jnp.where(slot < live, product, 0.0)
            total[core, 0, x, y, z] = total[core, 0, x, y, z] + product[:HALF]
            total[core, 1, x, y, z] = total[core, 1, x, y, z] + product[HALF:]

    loop(0, (live + UNROLL - 1) // UNROLL, some)

    def narrow(step):
        x, y = step // NY, step % NY
        for core in range(2):
            for half in range(2):
                out[core, half, x, y] = total[core, half, x, y].astype(jnp.bfloat16)

    loop(0, NX * NY, narrow)


def project_slab(values, columns, rows, count, basis):
    width = basis.shape[-1]
    smem = pl.BlockSpec(memory_space=pltpu.SMEM)
    vmem = pl.BlockSpec(memory_space=pltpu.VMEM)
    shape = (2, 2, NX, NY, NZ, HALF, width)
    return pl.pallas_call(
        project_kernel,
        out_shape=jax.ShapeDtypeStruct(shape, jnp.bfloat16),
        in_specs=[smem, smem, smem, vmem, vmem],
        out_specs=vmem,
        scratch_shapes=[pltpu.VMEM(shape, jnp.float32)],
        compiler_params=pltpu.CompilerParams(vmem_limit_bytes=VMEM_LIMIT),
        name="project_slab",
    )(columns, rows, count, values, basis)


GROUP = 4


def factor_kernel(gram, upper, inverse, growth):
    size = gram.shape[0]
    tiles = size // 8
    lane = lax.broadcasted_iota(jnp.int32, (8, size), 1)
    sub = lax.broadcasted_iota(jnp.int32, (8, size), 0)
    left = [gram[8 * t : 8 * t + 8, :] for t in range(tiles)]
    right = [jnp.where(lane == sub + 8 * t, 1.0, 0.0).astype(jnp.float32) for t in range(tiles)]
    squares = jnp.zeros((8, size), jnp.float32)
    for t in range(tiles):
        squares = squares + jnp.where(lane == sub + 8 * t, left[t], 0.0)
    squares = jnp.sum(squares, axis=0, keepdims=True)
    for first in range(0, size, GROUP):
        home, base = first // 8, first % 8
        cols = [
            [jnp.broadcast_to(left[t][:, first + k : first + k + 1], (8, size)) for t in range(home, tiles)]
            for k in range(GROUP)
        ]
        pivot = [[cols[m][0][base + k : base + k + 1, :] for m in range(GROUP)] for k in range(GROUP)]
        row_left = [left[home][base + k : base + k + 1, :] for k in range(GROUP)]
        row_right = [right[home][base + k : base + k + 1, :] for k in range(GROUP)]
        for k in range(GROUP):
            over = 1.0 / pivot[k][k]
            for m in range(k + 1, GROUP):
                factor = pivot[k][m] * over
                for n in range(m, GROUP):
                    pivot[m][n] = pivot[m][n] - factor * pivot[k][n]
                row_left[m] = row_left[m] - factor * row_left[k]
                row_right[m] = row_right[m] - factor * row_right[k]
                cols[m] = [c - b * factor for c, b in zip(cols[m], cols[k])]
            row_left[k] = row_left[k] * over
            row_right[k] = row_right[k] * over
        for k in range(GROUP):
            cols[k][0] = jnp.where(sub > base + k, cols[k][0], 0.0)
        for t in range(home, tiles):
            for k in range(GROUP):
                left[t] = left[t] - cols[k][t - home] * row_left[k]
                right[t] = right[t] - cols[k][t - home] * row_right[k]
    spread = jnp.zeros((8, size), jnp.float32)
    for t in range(tiles):
        diagonal = jnp.sum(jnp.where(lane == sub + 8 * t, left[t], 0.0), axis=1, keepdims=True)
        over = 1.0 / jnp.sqrt(diagonal)
        upper[8 * t : 8 * t + 8, :] = jnp.where(lane >= sub + 8 * t, left[t] * over, 0.0)
        row = right[t] * over
        inverse[8 * t : 8 * t + 8, :] = row
        spread = spread + row * row * squares
    growth[0, 0] = jnp.sum(spread) * (1.0 / size)


def factor(gram):
    shape = jax.ShapeDtypeStruct(gram.shape, jnp.float32)
    vmem = pl.BlockSpec(memory_space=pltpu.VMEM)
    return pl.pallas_call(
        factor_kernel,
        out_shape=(shape, shape, jax.ShapeDtypeStruct((1, 1), jnp.float32)),
        in_specs=[vmem],
        out_specs=(vmem, vmem, pl.BlockSpec(memory_space=pltpu.SMEM)),
        name="factor",
    )(gram)


def full_dot(left, right, contract):
    return lax.dot_general(
        left, right, ((contract[:1], contract[1:]), ((), ())), precision=precise, preferred_element_type=jnp.float32
    )


def right_divide(row_block, lower_part):
    return lax.linalg.triangular_solve(
        lower_part, row_block, left_side=False, lower=True, transpose_a=True
    )


GROWTH_LIMIT = 2.0


def on_device(block_values, block_rows, block_cols, block_count, test_matrix):
    slot_count, width_block, _ = block_values.shape
    sketch_width = test_matrix.shape[1]
    slab_total = lax.axis_size("wide") * lax.axis_size("narrow")
    slab_index = lax.axis_index(AXES)
    local_rows = block_rows - slab_index * RB_DEV
    omega = gather_rows(test_matrix)
    sketch, gram, share = slab_products(block_values, block_cols, local_rows, block_count, omega)
    sketch = sketch.reshape(RB_DEV * width_block, sketch_width)
    total_rows = sketch.shape[0] * slab_total
    row_scale = math.sqrt(total_rows)
    column_scale = math.sqrt(NCOL / (slot_count * slab_total * width_block))
    summed, whole = scatter_shares(share, gram, 1)
    upper, inverse, growth = factor(whole)

    def one_pass(sketch, summed, whole, upper, inverse):
        q_basis = (full_dot(sketch, inverse, (1, 1)) * row_scale).astype(jnp.bfloat16)
        projected = full_dot(summed, inverse, (1, 1)) * (row_scale * column_scale)
        return q_basis, upper / row_scale, projected

    def two_passes(sketch, summed, whole, upper, inverse):
        lower_one = jnp.linalg.cholesky(whole)
        first_basis = right_divide(sketch, lower_one)
        second_gram = full_dot(first_basis, first_basis, (0, 0))
        lower_two = jnp.linalg.cholesky(total_over_devices(second_gram, 2))
        q_basis = (right_divide(first_basis, lower_two) * row_scale).astype(jnp.bfloat16)
        r_factor = full_dot(lower_one, lower_two, (1, 0)).T / row_scale
        basis_blocks = q_basis.reshape(RB_DEV, width_block, sketch_width)
        basis_share = project_slab(block_values, block_cols, local_rows, block_count, basis_blocks)
        projected, _ = scatter_shares(basis_share, second_gram, 3)
        return q_basis, r_factor, projected * column_scale

    return lax.cond(
        growth[0, 0] <= GROWTH_LIMIT, one_pass, two_passes, sketch, summed, whole, upper, inverse
    )


def solution(mesh):
    placed = (
        P(AXES, None, None),
        P(AXES),
        P(AXES),
        P(AXES),
        P(AXES, None),
    )
    return jax.shard_map(
        on_device,
        mesh=mesh,
        in_specs=placed,
        out_specs=(P(AXES, None), P(), P(AXES, None)),
        check_vma=False,
    )
```

```python
import math

import jax
import jax.numpy as jnp
from jax import lax
from jax.experimental import pallas as pl
from jax.experimental.pallas import tpu as pltpu
from jax.sharding import PartitionSpec as P

NCOL = 32768
RB_DEV = 16
BLOCK = 128
HALF = 64
QUARTER = 32
NX, NY, NZ = 4, 4, 8

MESH = pl.DeviceIdType.MESH
AXES = ("wide", "narrow")
VMEM_LIMIT = 52 * 1024 * 1024

precise = lax.Precision.HIGHEST


def place():
    wide = lax.axis_index("wide")
    narrow = lax.axis_index("narrow")
    return narrow // NY, narrow % NY, wide // 2, wide % 2


def at(x, y, z, core):
    return (z * 2 + core, x * NY + y)


def column_place(column):
    narrow = column % (NX * NY)
    wide = column // (NX * NY)
    return wide % 2, narrow // NY, narrow % NY, wide // 2


def loop(low, high, body):
    def step(index, carry):
        body(index)
        return carry

    lax.fori_loop(low, high, step, 0)


def greet_torus(x, y, z, core):
    barrier = pltpu.get_barrier_semaphore()

    def greet(device):
        pl.semaphore_signal(barrier, inc=1, device_id=device, device_id_type=MESH)

    loop(1, NX, lambda k: greet(at((x + k) % NX, y, z, core)))
    loop(1, NY, lambda k: greet(at(x, (y + k) % NY, z, core)))
    loop(1, NZ, lambda k: greet(at(x, y, (z + k) % NZ, core)))
    greet(at(x, y, z, 1 - core))
    pl.semaphore_wait(barrier, NX + NY + NZ - 2)


def remote(src, dst, send, recv, device):
    return pltpu.make_async_remote_copy(
        src_ref=src, dst_ref=dst, send_sem=send, recv_sem=recv, device_id=device, device_id_type=MESH
    )


def gather_kernel(mine, out, local_sem, sz, rz, sx, rx, sy, ry, sn, rn, sf, rf, sc, rc):
    x, y, z, core = place()
    home = out.at[core, :, x, y, z]
    greet_torus(x, y, z, core)
    keep = pltpu.make_async_copy(mine, home, local_sem)
    keep.start()

    def along_z(k):
        return remote(mine, home, sz.at[k], rz.at[k], at(x, y, (z + k) % NZ, core))

    loop(1, NZ, lambda k: along_z(k).start())
    keep.wait()
    loop(1, NZ, lambda k: along_z(k).wait())

    def first_x(k):
        piece = out.at[core, 0, x, y]
        return remote(piece, piece, sx.at[k], rx.at[k], at((x + k) % NX, y, z, core))

    def first_y(k):
        piece = out.at[core, 1, x, y]
        return remote(piece, piece, sy.at[k], ry.at[k], at(x, (y + k) % NY, z, core))

    loop(1, NX, lambda k: first_x(k).start())
    loop(1, NY, lambda k: first_y(k).start())

    def piece(kind, back, half):
        if kind == 0:
            return out.at[core, 0, pl.ds(2 * half, 2), (y + NY - back) % NY]
        return out.at[core, 1, (x + NX - back) % NX, pl.ds(2 * half, 2)]

    def beside(kind, side):
        step = 3 if side else 1
        if kind == 0:
            return at(x, (y + step) % NY, z, core)
        return at((x + step) % NX, y, z, core)

    def near(kind, side, half):
        part = piece(kind, 0, half)
        return remote(part, part, sn.at[kind, side, half], rn.at[kind, side, half], beside(kind, side))

    def far(kind, side):
        part = piece(kind, 3 if side else 1, side)
        return remote(part, part, sf.at[kind, side], rf.at[kind, side], beside(kind, side))

    def across(kind, back, half):
        part = piece(kind, back, half)
        return remote(part, part, sc.at[kind, back, half], rc.at[kind, back, half], at(x, y, z, 1 - core))

    def begin(kind):
        for turn in range(2):
            near(kind, 0, turn).start()
            near(kind, 1, 1 - turn).start()

    loop(1, NX, lambda k: first_x(k).wait())
    begin(0)
    loop(1, NY, lambda k: first_y(k).wait())
    begin(1)
    for kind in range(2):
        for half in range(2):
            across(kind, 0, half).start()
    for kind in range(2):
        for side in range(2):
            near(kind, side, side).wait_recv()
            far(kind, side).start()
            across(kind, 3 if side else 1, side).start()
    for kind in range(2):
        for side in range(2):
            near(kind, side, 1 - side).wait_recv()
            across(kind, 3 if side else 1, 1 - side).start()
    for kind in range(2):
        for side in range(2):
            far(kind, side).wait_recv()
            across(kind, 2, side).start()
    for kind in range(2):
        for side in range(2):
            for half in range(2):
                near(kind, side, half).wait_send()
            far(kind, side).wait_send()
        for back in range(4):
            for half in range(2):
                across(kind, back, half).wait()


def gather_rows(test_matrix):
    width = test_matrix.shape[1]
    dma = pltpu.SemaphoreType.DMA
    return pl.pallas_call(
        gather_kernel,
        out_shape=jax.ShapeDtypeStruct((2, 2, NX, NY, NZ, HALF, width), jnp.bfloat16),
        in_specs=[pl.BlockSpec(memory_space=pl.ANY)],
        out_specs=pl.BlockSpec(memory_space=pl.ANY),
        scratch_shapes=[
            dma,
            dma((NZ,)),
            dma((NZ,)),
            dma((NX,)),
            dma((NX,)),
            dma((NY,)),
            dma((NY,)),
            dma((2, 2, 2)),
            dma((2, 2, 2)),
            dma((2, 2)),
            dma((2, 2)),
            dma((2, 4, 2)),
            dma((2, 4, 2)),
        ],
        compiler_params=pltpu.CompilerParams(collective_id=0, has_side_effects=True),
        name="gather_rows",
    )(test_matrix.reshape(2, HALF, width))


class gram_steps:
    def __init__(self, part, out, got, mid, got_wide, s1, r1, s2, r2, s3, r3):
        self.part, self.out, self.got, self.mid, self.got_wide = part, out, got, mid, got_wide
        self.s1, self.r1, self.s2, self.r2, self.s3, self.r3 = s1, r1, s2, r2, s3, r3
        self.wide, self.narrow = lax.axis_index("wide"), lax.axis_index("narrow")
        self.wides, self.narrows = 2 * NZ, NX * NY
        self.rows = part.shape[0] // self.narrows

    def greet(self):
        wide, narrow, wides, narrows = self.wide, self.narrow, self.wides, self.narrows
        barrier = pltpu.get_barrier_semaphore()

        def one(device):
            pl.semaphore_signal(barrier, inc=1, device_id=device, device_id_type=MESH)

        loop(1, narrows, lambda k: one((wide, (narrow + k) % narrows)))
        loop(1, wides, lambda k: one(((wide + k) % wides, narrow)))
        pl.semaphore_wait(barrier, narrows + wides - 2)

    def chunk(self, ref, index):
        return ref.at[pl.ds(pl.multiple_of(index * self.rows, self.rows), self.rows)]

    def scatter(self, k):
        peer = (self.narrow + k) % self.narrows
        source = self.chunk(self.part, peer)
        return remote(source, self.got.at[self.narrow], self.s1.at[k], self.r1.at[k], (self.wide, peer))

    def exchange(self, k):
        device = ((self.wide + k) % self.wides, self.narrow)
        return remote(self.mid, self.got_wide.at[self.wide], self.s2.at[k], self.r2.at[k], device)

    def spread(self, k):
        piece = self.chunk(self.out, self.narrow)
        device = (self.wide, (self.narrow + k) % self.narrows)
        return remote(piece, piece, self.s3.at[k], self.r3.at[k], device)

    def scatter_start(self):
        loop(1, self.narrows, lambda k: self.scatter(k).start())
        self.got[self.narrow] = self.chunk(self.part, self.narrow)[...]

    def scatter_finish(self):
        loop(1, self.narrows, lambda k: self.scatter(k).wait())
        total = self.got[0]
        for index in range(1, self.narrows):
            total = total + self.got[index]
        self.mid[...] = total
        self.got_wide[self.wide] = total
        loop(1, self.wides, lambda k: self.exchange(k).start())

    def exchange_finish(self):
        loop(1, self.wides, lambda k: self.exchange(k).wait())
        total = self.got_wide[0]
        for index in range(1, self.wides):
            total = total + self.got_wide[index]
        self.chunk(self.out, self.narrow)[...] = total
        loop(1, self.narrows, lambda k: self.spread(k).start())

    def spread_finish(self):
        loop(1, self.narrows, lambda k: self.spread(k).wait())


def total_kernel(part, out, got, mid, got_wide, s1, r1, s2, r2, s3, r3):
    gram = gram_steps(part, out, got, mid, got_wide, s1, r1, s2, r2, s3, r3)
    gram.greet()
    gram.scatter_start()
    gram.scatter_finish()
    gram.exchange_finish()
    gram.spread_finish()


def total_over_devices(matrix, collective_id):
    narrows, wides = NX * NY, 2 * NZ
    rows, width = matrix.shape[0] // narrows, matrix.shape[1]
    dma = pltpu.SemaphoreType.DMA
    return pl.pallas_call(
        total_kernel,
        out_shape=jax.ShapeDtypeStruct(matrix.shape, jnp.float32),
        in_specs=[pl.BlockSpec(memory_space=pltpu.VMEM)],
        out_specs=pl.BlockSpec(memory_space=pltpu.VMEM),
        scratch_shapes=[
            pltpu.VMEM((narrows, rows, width), jnp.float32),
            pltpu.VMEM((rows, width), jnp.float32),
            pltpu.VMEM((wides, rows, width), jnp.float32),
            dma((narrows,)),
            dma((narrows,)),
            dma((wides,)),
            dma((wides,)),
            dma((narrows,)),
            dma((narrows,)),
        ],
        compiler_params=pltpu.CompilerParams(collective_id=collective_id, has_side_effects=True),
        name="total_gram",
    )(matrix)


def scatter_kernel(
    share, part, out, whole, own, got, far_in, near_in, pair, cross_in, last, z_in, got_narrow, mid, got_wide,
    so, sc, rc, sf, rf, sn, rn, sb, rb, sz, rz, s1, r1, s2, r2, s3, r3,
):
    x, y, z, core = place()
    other = 1 - core
    f32, bf16 = jnp.float32, jnp.bfloat16
    gram = gram_steps(part, whole, got_narrow, mid, got_wide, s1, r1, s2, r2, s3, r3)

    def along(kind, step):
        if kind == 0:
            return at((x + step) % NX, y, z, core)
        return at(x, (y + step) % NY, z, core)

    def chunk(ref, kind, duo, step):
        if kind == 0:
            return ref.at[2 * duo, (x + step) % NX]
        return ref.at[2 * duo + 1, :, (y + step) % NY]

    def half_of(ref, kind, duo, step, half):
        if kind == 0:
            return ref.at[2 * duo, (x + step) % NX, pl.ds(2 * half, 2)]
        return ref.at[2 * duo + 1, pl.ds(2 * half, 2), (y + step) % NY]

    def line(ref, kind, duo, step, index):
        if kind == 0:
            return ref.at[2 * duo, (x + step) % NX, index]
        return ref.at[2 * duo + 1, index, (y + step) % NY]

    def mine(kind, duo, step):
        source = chunk(share.at[core], kind, duo, step)
        return pltpu.make_async_copy(source, chunk(own, kind, duo, step), so.at[kind, duo, step])

    def across(kind, duo, step):
        source, target = chunk(share.at[other], kind, duo, step), chunk(got, kind, duo, step)
        return remote(source, target, sc.at[kind, duo, step], rc.at[kind, duo, step], at(x, y, z, other))

    def far(kind, duo, side):
        source = half_of(own, kind, duo, 2, side)
        return remote(
            source, far_in.at[kind, duo, side], sf.at[kind, duo, side], rf.at[kind, duo, side],
            along(kind, 3 if side else 1),
        )

    def near(kind, duo, side, half):
        step = 3 if side else 1
        source = half_of(own, kind, duo, step, half)
        target = near_in.at[kind, duo, side, pl.ds(2 * half, 2)]
        return remote(
            source, target, sn.at[kind, duo, side, half], rn.at[kind, duo, side, half], along(kind, step)
        )

    def cross(kind, duo, k):
        to = (y + k) % NY if kind == 0 else (x + k) % NX
        return remote(
            pair.at[kind, duo, to], cross_in.at[kind, duo, k - 1], sb.at[kind, duo, k], rb.at[kind, duo, k],
            along(1 - kind, k),
        )

    def third(duo, k):
        to = (z + k) % NZ
        return remote(
            last.at[duo, to], z_in.at[duo, k - 1], sz.at[duo, k], rz.at[duo, k], at(x, y, to, core)
        )

    order = (2, 1, 3, 0)

    def bring(duo):
        for step in order:
            for kind in range(2):
                mine(kind, duo, step).start()

    def send_over(duo):
        for step in order:
            for kind in range(2):
                across(kind, duo, step).start()

    def join(kind, duo, step):
        mine(kind, duo, step).wait()
        across(kind, duo, step).wait_recv()

        def add(index):
            a, b = line(own, kind, duo, step, index), line(got, kind, duo, step, index)
            a[...] = (a[...].astype(f32) + b[...].astype(f32)).astype(bf16)

        loop(0, 4, add)

    def first(duo):
        for kind in range(2):
            join(kind, duo, 2)
            far(kind, duo, 0).start()
            far(kind, duo, 1).start()
        for kind in range(2):
            for side in range(2):
                join(kind, duo, 3 if side else 1)
                near(kind, duo, side, 1 - side).start()
        for kind in range(2):
            for side in range(2):
                far(kind, duo, side).wait_recv()

                def add(index):
                    a = line(own, kind, duo, 3 if side else 1, 2 * side + index)
                    a[...] = (a[...].astype(f32) + far_in[kind, duo, side, index].astype(f32)).astype(bf16)

                loop(0, 2, add)
                near(kind, duo, side, side).start()
        for kind in range(2):
            join(kind, duo, 0)

    def second(duo):
        for kind in range(2):
            for side in range(2):
                for half in range(2):
                    near(kind, duo, side, half).wait_recv()

            def add(index):
                total = line(own, kind, duo, 0, index)[...].astype(f32)
                total = total + near_in[kind, duo, 0, index].astype(f32)
                total = total + near_in[kind, duo, 1, index].astype(f32)
                pair[kind, duo, index] = total.astype(bf16)

            loop(0, 4, add)
            loop(1, 4, lambda k: cross(kind, duo, k).start())

    def final(duo):
        for kind in range(2):
            loop(1, 4, lambda k: cross(kind, duo, k).wait_recv())

        def add(index):
            for kind in range(2):
                total = pair[kind, duo, y if kind == 0 else x, index].astype(f32)
                for k in range(3):
                    total = total + cross_in[kind, duo, k, index].astype(f32)
                last[duo, index, kind] = total.astype(bf16)

        loop(0, NZ, add)
        loop(1, NZ, lambda k: third(duo, k).start())

    def finish(duo):
        loop(1, NZ, lambda k: third(duo, k).wait_recv())
        total = last[duo, z].astype(f32)
        for k in range(NZ - 1):
            total = total + z_in[duo, k].astype(f32)
        out[duo] = total

    def drain(duo):
        for kind in range(2):
            loop(0, 4, lambda step: across(kind, duo, step).wait_send())
            for side in range(2):
                far(kind, duo, side).wait_send()
                for half in range(2):
                    near(kind, duo, side, half).wait_send()
            loop(1, 4, lambda k: cross(kind, duo, k).wait_send())
        loop(1, NZ, lambda k: third(duo, k).wait_send())

    loop(0, 2, bring)
    gram.greet()
    gram.scatter_start()
    loop(0, 2, send_over)
    loop(0, 2, first)
    gram.scatter_finish()
    gram.exchange_finish()
    loop(0, 2, second)
    loop(0, 2, final)
    gram.spread_finish()
    loop(0, 2, finish)
    loop(0, 2, drain)


def scatter_shares(share, gram, collective_id):
    width = share.shape[-1]
    bf16 = jnp.bfloat16
    dma = pltpu.SemaphoreType.DMA
    tail = (NZ, QUARTER, width)
    vmem = pltpu.VMEM
    narrows, wides = NX * NY, 2 * NZ
    rows = gram.shape[0] // narrows
    in_vmem = pl.BlockSpec(memory_space=pltpu.VMEM)
    summed, whole = pl.pallas_call(
        scatter_kernel,
        out_shape=(
            jax.ShapeDtypeStruct((2, 2, QUARTER, width), jnp.float32),
            jax.ShapeDtypeStruct(gram.shape, jnp.float32),
        ),
        in_specs=[pl.BlockSpec(memory_space=pl.ANY), in_vmem],
        out_specs=(in_vmem, in_vmem),
        scratch_shapes=[
            vmem((4, NX, NY, *tail), bf16),
            vmem((4, NX, NY, *tail), bf16),
            vmem((2, 2, 2, 2, *tail), bf16),
            vmem((2, 2, 2, 4, *tail), bf16),
            vmem((2, 2, 4, *tail), bf16),
            vmem((2, 2, 3, *tail), bf16),
            vmem((2, NZ, 2, QUARTER, width), bf16),
            vmem((2, NZ - 1, 2, QUARTER, width), bf16),
            vmem((narrows, rows, width), jnp.float32),
            vmem((rows, width), jnp.float32),
            vmem((wides, rows, width), jnp.float32),
            dma((2, 2, 4)),
            dma((2, 2, 4)),
            dma((2, 2, 4)),
            dma((2, 2, 2)),
            dma((2, 2, 2)),
            dma((2, 2, 2, 2)),
            dma((2, 2, 2, 2)),
            dma((2, 2, 4)),
            dma((2, 2, 4)),
            dma((2, NZ)),
            dma((2, NZ)),
            dma((narrows,)),
            dma((narrows,)),
            dma((wides,)),
            dma((wides,)),
            dma((narrows,)),
            dma((narrows,)),
        ],
        compiler_params=pltpu.CompilerParams(
            collective_id=collective_id, has_side_effects=True, vmem_limit_bytes=VMEM_LIMIT
        ),
        name="scatter_shares",
    )(share, gram)
    return summed.reshape(4 * QUARTER, width), whole


UNROLL = 4


def slab_kernel(
    columns, rows, count, values_hbm, omega_hbm, sketch, gram, share,
    values, omega, blank, totals, packed, rounded, seen, first, sv, so, sb, sw,
):
    live = count[0]
    steps = (live + UNROLL - 1) // UNROLL
    bring_values = pltpu.make_async_copy(values_hbm, values, sv)
    bring_omega = pltpu.make_async_copy(omega_hbm, omega, so)
    bring_omega.start()
    bring_values.start()
    sketch[...] = jnp.zeros_like(sketch)

    def clear(x):
        blank[x] = jnp.zeros(blank.shape[1:], jnp.bfloat16)

    loop(0, NX, clear)

    def unseen(step):
        for u in range(8):
            seen[step * 8 + u] = -1

    loop(0, seen.shape[0] // 8, unseen)

    def number(slot):
        first[slot] = slot

    loop(0, first.shape[0], number)

    def look(slot):
        before = seen[columns[slot]]
        chosen = jnp.where(before < 0, slot, before)
        seen[columns[slot]] = chosen
        first[slot] = chosen

    loop(0, live, look)
    bring_omega.wait()
    bring_values.wait()

    def wipe(core, quarter):
        return pltpu.make_async_copy(blank, share.at[core, quarter], sb.at[core, quarter])

    for core in range(2):
        for quarter in range(4):
            wipe(core, quarter).start()

    def add_sketch(step):
        products = []
        for u in range(UNROLL):
            slot = step * UNROLL + u
            core, x, y, z = column_place(columns[slot])
            picked = jnp.concatenate([omega[core, 0, x, y, z], omega[core, 1, x, y, z]], axis=0)
            products.append(jnp.dot(values[slot], picked, preferred_element_type=jnp.float32))
        for u in range(UNROLL):
            slot = step * UNROLL + u
            row = rows[slot] % RB_DEV
            sketch[row] = sketch[row] + jnp.where(slot < live, products[u], 0.0)

    loop(0, steps, add_sketch)
    gram[...] = jnp.zeros_like(gram)

    def add_gram(step):
        total = gram[...]
        for u in range(UNROLL):
            part = sketch[step * UNROLL + u]
            rounded[step * UNROLL + u] = part.astype(jnp.bfloat16)
            total = total + lax.dot_general(
                part, part, (((0,), (0,)), ((), ())), precision=precise, preferred_element_type=jnp.float32
            )
        gram[...] = total

    loop(0, sketch.shape[0] // UNROLL, add_gram)

    def add_share(step):
        products = []
        for u in range(UNROLL):
            slot = step * UNROLL + u
            products.append(
                lax.dot_general(
                    values[slot],
                    rounded[rows[slot] % RB_DEV],
                    (((0,), (0,)), ((), ())),
                    preferred_element_type=jnp.float32,
                )
            )
        for u in range(UNROLL):
            slot = step * UNROLL + u
            target = first[slot]
            totals[target] = jnp.where(target == slot, 0.0, totals[target]) + products[u]

    loop(0, steps, add_share)
    for core in range(2):
        for quarter in range(4):
            wipe(core, quarter).wait()

    def hand_out(slot):
        core, x, y, z = column_place(columns[slot])
        return pltpu.make_async_copy(packed.at[slot], share.at[core, :, x, y, z], sw.at[slot])

    def pack(slot):
        @pl.when(first[slot] == slot)
        def _():
            for quarter in range(4):
                rows_of = pl.ds(quarter * QUARTER, QUARTER)
                packed[slot, quarter] = totals[slot, rows_of].astype(jnp.bfloat16)
            hand_out(slot).start()

    loop(0, live, pack)

    def done(slot):
        @pl.when(first[slot] == slot)
        def _():
            hand_out(slot).wait()

    loop(0, live, done)


def slab_products(values, columns, rows, count, omega):
    slots = values.shape[0]
    width = omega.shape[-1]
    smem = pl.BlockSpec(memory_space=pltpu.SMEM)
    vmem = pl.BlockSpec(memory_space=pltpu.VMEM)
    hbm = pl.BlockSpec(memory_space=pl.ANY)
    dma = pltpu.SemaphoreType.DMA
    f32, bf16 = jnp.float32, jnp.bfloat16
    return pl.pallas_call(
        slab_kernel,
        out_shape=(
            jax.ShapeDtypeStruct((RB_DEV, BLOCK, width), f32),
            jax.ShapeDtypeStruct((width, width), f32),
            jax.ShapeDtypeStruct((2, 4, NX, NY, NZ, QUARTER, width), bf16),
        ),
        in_specs=[smem, smem, smem, hbm, hbm],
        out_specs=(vmem, vmem, hbm),
        scratch_shapes=[
            pltpu.VMEM(values.shape, bf16),
            pltpu.VMEM(omega.shape, bf16),
            pltpu.VMEM((NX, NY, NZ, QUARTER, width), bf16),
            pltpu.VMEM((slots, BLOCK, width), f32),
            pltpu.VMEM((slots, 4, QUARTER, width), bf16),
            pltpu.VMEM((RB_DEV, BLOCK, width), bf16),
            pltpu.SMEM((NCOL // BLOCK,), jnp.int32),
            pltpu.SMEM((slots,), jnp.int32),
            dma,
            dma,
            dma((2, 4)),
            dma((slots,)),
        ],
        compiler_params=pltpu.CompilerParams(vmem_limit_bytes=VMEM_LIMIT),
        name="slab_products",
    )(columns, rows, count, values, omega)


def project_kernel(columns, rows, count, values, basis, out, total):
    live = count[0]

    def clear(step):
        for core in range(2):
            for quarter in range(4):
                total[core, quarter, step // NY, step % NY] = jnp.zeros(total.shape[4:], jnp.float32)

    loop(0, NX * NY, clear)

    def some(step):
        for u in range(UNROLL):
            slot = step * UNROLL + u
            core, x, y, z = column_place(columns[slot])
            product = lax.dot_general(
                values[slot], basis[rows[slot] % RB_DEV], (((0,), (0,)), ((), ())), preferred_element_type=jnp.float32
            )
            product = jnp.where(slot < live, product, 0.0)
            for quarter in range(4):
                piece = product[quarter * QUARTER : (quarter + 1) * QUARTER]
                total[core, quarter, x, y, z] = total[core, quarter, x, y, z] + piece

    loop(0, (live + UNROLL - 1) // UNROLL, some)

    def narrow(step):
        x, y = step // NY, step % NY
        for core in range(2):
            for quarter in range(4):
                out[core, quarter, x, y] = total[core, quarter, x, y].astype(jnp.bfloat16)

    loop(0, NX * NY, narrow)


def project_slab(values, columns, rows, count, basis):
    width = basis.shape[-1]
    smem = pl.BlockSpec(memory_space=pltpu.SMEM)
    vmem = pl.BlockSpec(memory_space=pltpu.VMEM)
    shape = (2, 4, NX, NY, NZ, QUARTER, width)
    return pl.pallas_call(
        project_kernel,
        out_shape=jax.ShapeDtypeStruct(shape, jnp.bfloat16),
        in_specs=[smem, smem, smem, vmem, vmem],
        out_specs=vmem,
        scratch_shapes=[pltpu.VMEM(shape, jnp.float32)],
        compiler_params=pltpu.CompilerParams(vmem_limit_bytes=VMEM_LIMIT),
        name="project_slab",
    )(columns, rows, count, values, basis)


GROUP = 4


def factor_kernel(gram, upper, inverse, growth):
    size = gram.shape[0]
    tiles = size // 8
    lane = lax.broadcasted_iota(jnp.int32, (8, size), 1)
    sub = lax.broadcasted_iota(jnp.int32, (8, size), 0)
    left = [gram[8 * t : 8 * t + 8, :] for t in range(tiles)]
    right = [jnp.where(lane == sub + 8 * t, 1.0, 0.0).astype(jnp.float32) for t in range(tiles)]
    squares = jnp.zeros((8, size), jnp.float32)
    for t in range(tiles):
        squares = squares + jnp.where(lane == sub + 8 * t, left[t], 0.0)
    squares = jnp.sum(squares, axis=0, keepdims=True)
    for first in range(0, size, GROUP):
        home, base = first // 8, first % 8
        cols = [
            [jnp.broadcast_to(left[t][:, first + k : first + k + 1], (8, size)) for t in range(home, tiles)]
            for k in range(GROUP)
        ]
        pivot = [[cols[m][0][base + k : base + k + 1, :] for m in range(GROUP)] for k in range(GROUP)]
        row_left = [left[home][base + k : base + k + 1, :] for k in range(GROUP)]
        row_right = [right[home][base + k : base + k + 1, :] for k in range(GROUP)]
        for k in range(GROUP):
            over = 1.0 / pivot[k][k]
            for m in range(k + 1, GROUP):
                factor = pivot[k][m] * over
                for n in range(m, GROUP):
                    pivot[m][n] = pivot[m][n] - factor * pivot[k][n]
                row_left[m] = row_left[m] - factor * row_left[k]
                row_right[m] = row_right[m] - factor * row_right[k]
                cols[m] = [c - b * factor for c, b in zip(cols[m], cols[k])]
            row_left[k] = row_left[k] * over
            row_right[k] = row_right[k] * over
        for k in range(GROUP):
            cols[k][0] = jnp.where(sub > base + k, cols[k][0], 0.0)
        for t in range(home, tiles):
            for k in range(GROUP):
                left[t] = left[t] - cols[k][t - home] * row_left[k]
                right[t] = right[t] - cols[k][t - home] * row_right[k]
    spread = jnp.zeros((8, size), jnp.float32)
    for t in range(tiles):
        diagonal = jnp.sum(jnp.where(lane == sub + 8 * t, left[t], 0.0), axis=1, keepdims=True)
        over = 1.0 / jnp.sqrt(diagonal)
        upper[8 * t : 8 * t + 8, :] = jnp.where(lane >= sub + 8 * t, left[t] * over, 0.0)
        row = right[t] * over
        inverse[8 * t : 8 * t + 8, :] = row
        spread = spread + row * row * squares
    growth[0, 0] = jnp.sum(spread) * (1.0 / size)


def factor(gram):
    shape = jax.ShapeDtypeStruct(gram.shape, jnp.float32)
    vmem = pl.BlockSpec(memory_space=pltpu.VMEM)
    return pl.pallas_call(
        factor_kernel,
        out_shape=(shape, shape, jax.ShapeDtypeStruct((1, 1), jnp.float32)),
        in_specs=[vmem],
        out_specs=(vmem, vmem, pl.BlockSpec(memory_space=pltpu.SMEM)),
        name="factor",
    )(gram)


def full_dot(left, right, contract):
    return lax.dot_general(
        left, right, ((contract[:1], contract[1:]), ((), ())), precision=precise, preferred_element_type=jnp.float32
    )


def right_divide(row_block, lower_part):
    return lax.linalg.triangular_solve(
        lower_part, row_block, left_side=False, lower=True, transpose_a=True
    )


GROWTH_LIMIT = 2.0


def on_device(block_values, block_rows, block_cols, block_count, test_matrix):
    slot_count, width_block, _ = block_values.shape
    sketch_width = test_matrix.shape[1]
    slab_total = lax.axis_size("wide") * lax.axis_size("narrow")
    omega = gather_rows(test_matrix)
    sketch, gram, share = slab_products(block_values, block_cols, block_rows, block_count, omega)
    sketch = sketch.reshape(RB_DEV * width_block, sketch_width)
    total_rows = sketch.shape[0] * slab_total
    row_scale = math.sqrt(total_rows)
    column_scale = math.sqrt(NCOL / (slot_count * slab_total * width_block))
    summed, whole = scatter_shares(share, gram, 1)
    upper, inverse, growth = factor(whole)

    def one_pass(sketch, summed, whole, upper, inverse):
        q_basis = (full_dot(sketch, inverse, (1, 1)) * row_scale).astype(jnp.bfloat16)
        projected = full_dot(summed, inverse, (1, 1)) * (row_scale * column_scale)
        return q_basis, upper / row_scale, projected

    def two_passes(sketch, summed, whole, upper, inverse):
        lower_one = jnp.linalg.cholesky(whole)
        first_basis = right_divide(sketch, lower_one)
        second_gram = full_dot(first_basis, first_basis, (0, 0))
        lower_two = jnp.linalg.cholesky(total_over_devices(second_gram, 2))
        q_basis = (right_divide(first_basis, lower_two) * row_scale).astype(jnp.bfloat16)
        r_factor = full_dot(lower_one, lower_two, (1, 0)).T / row_scale
        basis_blocks = q_basis.reshape(RB_DEV, width_block, sketch_width)
        basis_share = project_slab(block_values, block_cols, block_rows, block_count, basis_blocks)
        projected, _ = scatter_shares(basis_share, second_gram, 3)
        return q_basis, r_factor, projected * column_scale

    return lax.cond(
        growth[0, 0] <= GROWTH_LIMIT, one_pass, two_passes, sketch, summed, whole, upper, inverse
    )


def solution(mesh):
    placed = (
        P(AXES, None, None),
        P(AXES),
        P(AXES),
        P(AXES),
        P(AXES, None),
    )
    return jax.shard_map(
        on_device,
        mesh=mesh,
        in_specs=placed,
        out_specs=(P(AXES, None), P(), P(AXES, None)),
        check_vma=False,
    )
```

```python
import math

import jax
import jax.numpy as jnp
from jax import lax
from jax.experimental import pallas as pl
from jax.experimental.pallas import tpu as pltpu
from jax.sharding import PartitionSpec as P

NCOL = 32768
RB_DEV = 16
BLOCK = 128
QUARTER = 32
NX, NY, NZ = 4, 4, 8

MESH = pl.DeviceIdType.MESH
AXES = ("wide", "narrow")
VMEM_LIMIT = 52 * 1024 * 1024

precise = lax.Precision.HIGHEST


def place():
    wide = lax.axis_index("wide")
    narrow = lax.axis_index("narrow")
    return narrow // NY, narrow % NY, wide // 2, wide % 2


def at(x, y, z, core):
    return (z * 2 + core, x * NY + y)


def column_place(column):
    narrow = column % (NX * NY)
    wide = column // (NX * NY)
    return wide % 2, narrow // NY, narrow % NY, wide // 2


def loop(low, high, body):
    def step(index, carry):
        body(index)
        return carry

    lax.fori_loop(low, high, step, 0)


def greet_torus(x, y, z, core):
    barrier = pltpu.get_barrier_semaphore()

    def greet(device):
        pl.semaphore_signal(barrier, inc=1, device_id=device, device_id_type=MESH)

    loop(1, NX, lambda k: greet(at((x + k) % NX, y, z, core)))
    loop(1, NY, lambda k: greet(at(x, (y + k) % NY, z, core)))
    loop(1, NZ, lambda k: greet(at(x, y, (z + k) % NZ, core)))
    greet(at(x, y, z, 1 - core))
    pl.semaphore_wait(barrier, NX + NY + NZ - 2)


def remote(src, dst, send, recv, device):
    return pltpu.make_async_remote_copy(
        src_ref=src, dst_ref=dst, send_sem=send, recv_sem=recv, device_id=device, device_id_type=MESH
    )


def gather_kernel(mine, out, local_sem, sz, rz, sa, ra, sn, rn, sf, rf, sc, rc):
    x, y, z, core = place()
    greet_torus(x, y, z, core)
    keep = pltpu.make_async_copy(mine, out.at[core, :, x, y, z], local_sem)

    def along(kind, step):
        if kind == 0:
            return at((x + step) % NX, y, z, core)
        return at(x, (y + step) % NY, z, core)

    def along_z(duo, k):
        source = mine.at[pl.ds(2 * duo, 2)]
        target = out.at[core, pl.ds(2 * duo, 2), x, y, z]
        return remote(source, target, sz.at[duo, k], rz.at[duo, k], at(x, y, (z + k) % NZ, core))

    def first(kind, duo, k):
        part = out.at[core, 2 * duo + kind, x, y]
        return remote(part, part, sa.at[kind, duo, k], ra.at[kind, duo, k], along(kind, k))

    def piece(kind, duo, back, half):
        if kind == 0:
            return out.at[core, 2 * duo, pl.ds(2 * half, 2), (y + NY - back) % NY]
        return out.at[core, 2 * duo + 1, (x + NX - back) % NX, pl.ds(2 * half, 2)]

    def near(kind, duo, side, half):
        part = piece(kind, duo, 0, half)
        send, recv = sn.at[kind, duo, side, half], rn.at[kind, duo, side, half]
        return remote(part, part, send, recv, along(1 - kind, 3 if side else 1))

    def far(kind, duo, side):
        back = 3 if side else 1
        part = piece(kind, duo, back, side)
        return remote(part, part, sf.at[kind, duo, side], rf.at[kind, duo, side], along(1 - kind, back))

    def across(kind, duo, back, half):
        part = piece(kind, duo, back, half)
        send, recv = sc.at[kind, duo, back, half], rc.at[kind, duo, back, half]
        return remote(part, part, send, recv, at(x, y, z, 1 - core))

    def start_first(duo):
        loop(1, NZ, lambda k: along_z(duo, k).wait_recv())
        for k in range(1, 4):
            for kind in range(2):
                first(kind, duo, k).start()

    def start_near(duo):
        for kind in range(2):
            loop(1, 4, lambda k: first(kind, duo, k).wait_recv())
            for turn in range(2):
                near(kind, duo, 0, turn).start()
                near(kind, duo, 1, 1 - turn).start()
        for kind in range(2):
            for half in range(2):
                across(kind, duo, 0, half).start()

    def start_far(duo):
        for kind in range(2):
            for side in range(2):
                near(kind, duo, side, side).wait_recv()
                far(kind, duo, side).start()
                across(kind, duo, 3 if side else 1, side).start()

    def pass_near(duo):
        for kind in range(2):
            for side in range(2):
                near(kind, duo, side, 1 - side).wait_recv()
                across(kind, duo, 3 if side else 1, 1 - side).start()

    def pass_far(duo):
        for kind in range(2):
            for side in range(2):
                far(kind, duo, side).wait_recv()
                across(kind, duo, 2, side).start()

    def drain_early(duo):
        loop(1, NZ, lambda k: along_z(duo, k).wait_send())
        for kind in range(2):
            loop(1, 4, lambda k: first(kind, duo, k).wait_send())

    def drain(duo):
        for kind in range(2):
            for side in range(2):
                for half in range(2):
                    near(kind, duo, side, half).wait_send()
                far(kind, duo, side).wait_send()
            for back in range(4):
                for half in range(2):
                    across(kind, duo, back, half).wait()

    loop(1, NZ, lambda k: along_z(0, k).start())
    keep.start()
    loop(1, NZ, lambda k: along_z(1, k).start())
    keep.wait()
    loop(0, 2, start_first)
    loop(0, 2, start_near)
    start_far(0)
    pass_near(0)
    start_far(1)
    pass_near(1)
    loop(0, 2, drain_early)
    loop(0, 2, pass_far)
    loop(0, 2, drain)


def gather_rows(test_matrix):
    width = test_matrix.shape[1]
    dma = pltpu.SemaphoreType.DMA
    return pl.pallas_call(
        gather_kernel,
        out_shape=jax.ShapeDtypeStruct((2, 4, NX, NY, NZ, QUARTER, width), jnp.bfloat16),
        in_specs=[pl.BlockSpec(memory_space=pl.ANY)],
        out_specs=pl.BlockSpec(memory_space=pl.ANY),
        scratch_shapes=[
            dma,
            dma((2, NZ)),
            dma((2, NZ)),
            dma((2, 2, 4)),
            dma((2, 2, 4)),
            dma((2, 2, 2, 2)),
            dma((2, 2, 2, 2)),
            dma((2, 2, 2)),
            dma((2, 2, 2)),
            dma((2, 2, 4, 2)),
            dma((2, 2, 4, 2)),
        ],
        compiler_params=pltpu.CompilerParams(collective_id=0, has_side_effects=True),
        name="gather_rows",
    )(test_matrix.reshape(4, QUARTER, width))


class gram_steps:
    def __init__(self, part, out, got, mid, got_wide, s1, r1, s2, r2, s3, r3):
        self.part, self.out, self.got, self.mid, self.got_wide = part, out, got, mid, got_wide
        self.s1, self.r1, self.s2, self.r2, self.s3, self.r3 = s1, r1, s2, r2, s3, r3
        self.wide, self.narrow = lax.axis_index("wide"), lax.axis_index("narrow")
        self.wides, self.narrows = 2 * NZ, NX * NY
        self.rows = part.shape[0] // self.narrows

    def greet(self):
        wide, narrow, wides, narrows = self.wide, self.narrow, self.wides, self.narrows
        barrier = pltpu.get_barrier_semaphore()

        def one(device):
            pl.semaphore_signal(barrier, inc=1, device_id=device, device_id_type=MESH)

        loop(1, narrows, lambda k: one((wide, (narrow + k) % narrows)))
        loop(1, wides, lambda k: one(((wide + k) % wides, narrow)))
        pl.semaphore_wait(barrier, narrows + wides - 2)

    def chunk(self, ref, index):
        return ref.at[pl.ds(pl.multiple_of(index * self.rows, self.rows), self.rows)]

    def scatter(self, k):
        peer = (self.narrow + k) % self.narrows
        source = self.chunk(self.part, peer)
        return remote(source, self.got.at[self.narrow], self.s1.at[k], self.r1.at[k], (self.wide, peer))

    def exchange(self, k):
        device = ((self.wide + k) % self.wides, self.narrow)
        return remote(self.mid, self.got_wide.at[self.wide], self.s2.at[k], self.r2.at[k], device)

    def spread(self, k):
        piece = self.chunk(self.out, self.narrow)
        device = (self.wide, (self.narrow + k) % self.narrows)
        return remote(piece, piece, self.s3.at[k], self.r3.at[k], device)

    def scatter_start(self):
        loop(1, self.narrows, lambda k: self.scatter(k).start())
        self.got[self.narrow] = self.chunk(self.part, self.narrow)[...]

    def scatter_finish(self):
        loop(1, self.narrows, lambda k: self.scatter(k).wait_recv())
        total = self.got[0]
        for index in range(1, self.narrows):
            total = total + self.got[index]
        self.mid[...] = total
        self.got_wide[self.wide] = total
        loop(1, self.wides, lambda k: self.exchange(k).start())

    def exchange_finish(self):
        loop(1, self.wides, lambda k: self.exchange(k).wait_recv())
        total = self.got_wide[0]
        for index in range(1, self.wides):
            total = total + self.got_wide[index]
        self.chunk(self.out, self.narrow)[...] = total
        loop(1, self.narrows, lambda k: self.spread(k).start())

    def drain_early(self):
        loop(1, self.narrows, lambda k: self.scatter(k).wait_send())
        loop(1, self.wides, lambda k: self.exchange(k).wait_send())

    def spread_finish(self):
        loop(1, self.narrows, lambda k: self.spread(k).wait())


def total_kernel(part, out, got, mid, got_wide, s1, r1, s2, r2, s3, r3):
    gram = gram_steps(part, out, got, mid, got_wide, s1, r1, s2, r2, s3, r3)
    gram.greet()
    gram.scatter_start()
    gram.scatter_finish()
    gram.exchange_finish()
    gram.drain_early()
    gram.spread_finish()


def total_over_devices(matrix, collective_id):
    narrows, wides = NX * NY, 2 * NZ
    rows, width = matrix.shape[0] // narrows, matrix.shape[1]
    dma = pltpu.SemaphoreType.DMA
    return pl.pallas_call(
        total_kernel,
        out_shape=jax.ShapeDtypeStruct(matrix.shape, jnp.float32),
        in_specs=[pl.BlockSpec(memory_space=pltpu.VMEM)],
        out_specs=pl.BlockSpec(memory_space=pltpu.VMEM),
        scratch_shapes=[
            pltpu.VMEM((narrows, rows, width), jnp.float32),
            pltpu.VMEM((rows, width), jnp.float32),
            pltpu.VMEM((wides, rows, width), jnp.float32),
            dma((narrows,)),
            dma((narrows,)),
            dma((wides,)),
            dma((wides,)),
            dma((narrows,)),
            dma((narrows,)),
        ],
        compiler_params=pltpu.CompilerParams(collective_id=collective_id, has_side_effects=True),
        name="total_gram",
    )(matrix)


def scatter_kernel(
    share, part, out, whole, own, got, far_in, near_in, pair, cross_in, last, z_in, got_narrow, mid, got_wide,
    so, sc, rc, sf, rf, sn, rn, sb, rb, sz, rz, s1, r1, s2, r2, s3, r3,
):
    x, y, z, core = place()
    other = 1 - core
    f32, bf16 = jnp.float32, jnp.bfloat16
    gram = gram_steps(part, whole, got_narrow, mid, got_wide, s1, r1, s2, r2, s3, r3)

    def along(kind, step):
        if kind == 0:
            return at((x + step) % NX, y, z, core)
        return at(x, (y + step) % NY, z, core)

    def chunk(ref, kind, duo, step):
        if kind == 0:
            return ref.at[2 * duo, (x + step) % NX]
        return ref.at[2 * duo + 1, :, (y + step) % NY]

    def half_of(ref, kind, duo, step, half):
        if kind == 0:
            return ref.at[2 * duo, (x + step) % NX, pl.ds(2 * half, 2)]
        return ref.at[2 * duo + 1, pl.ds(2 * half, 2), (y + step) % NY]

    def line(ref, kind, duo, step, index):
        if kind == 0:
            return ref.at[2 * duo, (x + step) % NX, index]
        return ref.at[2 * duo + 1, index, (y + step) % NY]

    mine = pltpu.make_async_copy(share.at[core], own, so)

    def across(kind, duo, step):
        source, target = chunk(share.at[other], kind, duo, step), chunk(got, kind, duo, step)
        return remote(source, target, sc.at[kind, duo, step], rc.at[kind, duo, step], at(x, y, z, other))

    def far(kind, duo, side):
        source = half_of(own, kind, duo, 2, side)
        return remote(
            source, far_in.at[kind, duo, side], sf.at[kind, duo, side], rf.at[kind, duo, side],
            along(kind, 3 if side else 1),
        )

    def near(kind, duo, side, half):
        step = 3 if side else 1
        source = half_of(own, kind, duo, step, half)
        target = near_in.at[kind, duo, side, pl.ds(2 * half, 2)]
        return remote(
            source, target, sn.at[kind, duo, side, half], rn.at[kind, duo, side, half], along(kind, step)
        )

    def cross(kind, duo, k):
        to = (y + k) % NY if kind == 0 else (x + k) % NX
        return remote(
            pair.at[kind, duo, to], cross_in.at[kind, duo, k - 1], sb.at[kind, duo, k], rb.at[kind, duo, k],
            along(1 - kind, k),
        )

    def third(duo, k):
        to = (z + k) % NZ
        return remote(
            last.at[duo, to], z_in.at[duo, k - 1], sz.at[duo, k], rz.at[duo, k], at(x, y, to, core)
        )

    order = (2, 1, 3, 0)

    def send_over(duo):
        for step in order:
            for kind in range(2):
                across(kind, duo, step).start()

    def join(kind, duo, step):
        across(kind, duo, step).wait_recv()

        def add(index):
            a, b = line(own, kind, duo, step, index), line(got, kind, duo, step, index)
            a[...] = (a[...].astype(f32) + b[...].astype(f32)).astype(bf16)

        loop(0, 4, add)

    def first(duo):
        for kind in range(2):
            join(kind, duo, 2)
            far(kind, duo, 0).start()
            far(kind, duo, 1).start()
        for kind in range(2):
            for side in range(2):
                join(kind, duo, 3 if side else 1)
                near(kind, duo, side, 1 - side).start()
        for kind in range(2):
            for side in range(2):
                far(kind, duo, side).wait_recv()

                def add(index):
                    a = line(own, kind, duo, 3 if side else 1, 2 * side + index)
                    a[...] = (a[...].astype(f32) + far_in[kind, duo, side, index].astype(f32)).astype(bf16)

                loop(0, 2, add)
                near(kind, duo, side, side).start()
        for kind in range(2):
            join(kind, duo, 0)

    def second(duo):
        for kind in range(2):
            for side in range(2):
                for half in range(2):
                    near(kind, duo, side, half).wait_recv()

            def add(index):
                total = line(own, kind, duo, 0, index)[...].astype(f32)
                total = total + near_in[kind, duo, 0, index].astype(f32)
                total = total + near_in[kind, duo, 1, index].astype(f32)
                pair[kind, duo, index] = total.astype(bf16)

            loop(0, 4, add)
            loop(1, 4, lambda k: cross(kind, duo, k).start())

    def final(duo):
        for kind in range(2):
            loop(1, 4, lambda k: cross(kind, duo, k).wait_recv())

        def add(index):
            for kind in range(2):
                total = pair[kind, duo, y if kind == 0 else x, index].astype(f32)
                for k in range(3):
                    total = total + cross_in[kind, duo, k, index].astype(f32)
                last[duo, index, kind] = total.astype(bf16)

        loop(0, NZ, add)
        loop(1, NZ, lambda k: third(duo, k).start())

    def finish(duo):
        loop(1, NZ, lambda k: third(duo, k).wait_recv())
        total = last[duo, z].astype(f32)
        for k in range(NZ - 1):
            total = total + z_in[duo, k].astype(f32)
        out[duo] = total

    def drain_first(duo):
        for kind in range(2):
            loop(0, 4, lambda step: across(kind, duo, step).wait_send())
            for side in range(2):
                far(kind, duo, side).wait_send()

    def drain_second(duo):
        for kind in range(2):
            for side in range(2):
                for half in range(2):
                    near(kind, duo, side, half).wait_send()
            loop(1, 4, lambda k: cross(kind, duo, k).wait_send())

    mine.start()
    gram.greet()
    loop(0, 2, send_over)
    gram.scatter_start()
    mine.wait()
    loop(0, 2, first)
    gram.scatter_finish()
    gram.exchange_finish()
    loop(0, 2, second)
    loop(0, 2, drain_first)
    gram.drain_early()
    loop(0, 2, final)
    loop(0, 2, drain_second)
    gram.spread_finish()
    loop(0, 2, finish)
    loop(0, 2, lambda duo: loop(1, NZ, lambda k: third(duo, k).wait_send()))


def scatter_shares(share, gram, collective_id):
    width = share.shape[-1]
    bf16 = jnp.bfloat16
    dma = pltpu.SemaphoreType.DMA
    tail = (NZ, QUARTER, width)
    vmem = pltpu.VMEM
    narrows, wides = NX * NY, 2 * NZ
    rows = gram.shape[0] // narrows
    in_vmem = pl.BlockSpec(memory_space=pltpu.VMEM)
    summed, whole = pl.pallas_call(
        scatter_kernel,
        out_shape=(
            jax.ShapeDtypeStruct((2, 2, QUARTER, width), jnp.float32),
            jax.ShapeDtypeStruct(gram.shape, jnp.float32),
        ),
        in_specs=[pl.BlockSpec(memory_space=pl.ANY), in_vmem],
        out_specs=(in_vmem, in_vmem),
        scratch_shapes=[
            vmem((4, NX, NY, *tail), bf16),
            vmem((4, NX, NY, *tail), bf16),
            vmem((2, 2, 2, 2, *tail), bf16),
            vmem((2, 2, 2, 4, *tail), bf16),
            vmem((2, 2, 4, *tail), bf16),
            vmem((2, 2, 3, *tail), bf16),
            vmem((2, NZ, 2, QUARTER, width), bf16),
            vmem((2, NZ - 1, 2, QUARTER, width), bf16),
            vmem((narrows, rows, width), jnp.float32),
            vmem((rows, width), jnp.float32),
            vmem((wides, rows, width), jnp.float32),
            dma,
            dma((2, 2, 4)),
            dma((2, 2, 4)),
            dma((2, 2, 2)),
            dma((2, 2, 2)),
            dma((2, 2, 2, 2)),
            dma((2, 2, 2, 2)),
            dma((2, 2, 4)),
            dma((2, 2, 4)),
            dma((2, NZ)),
            dma((2, NZ)),
            dma((narrows,)),
            dma((narrows,)),
            dma((wides,)),
            dma((wides,)),
            dma((narrows,)),
            dma((narrows,)),
        ],
        compiler_params=pltpu.CompilerParams(
            collective_id=collective_id, has_side_effects=True, vmem_limit_bytes=VMEM_LIMIT
        ),
        name="scatter_shares",
    )(share, gram)
    return summed.reshape(4 * QUARTER, width), whole


UNROLL = 16


def slab_kernel(
    columns, rows, count, values_hbm, omega_hbm, sketch, gram, share,
    values, omega, blank, totals, packed, rounded, seen, first, sv, so, sb, sw,
):
    live = count[0]
    steps = (live + UNROLL - 1) // UNROLL
    bring_values = pltpu.make_async_copy(values_hbm, values, sv)

    def bring(slot):
        core, x, y, z = column_place(columns[slot])
        return pltpu.make_async_copy(omega_hbm.at[core, :, x, y, z], omega.at[slot], so.at[slot])

    bring_values.start()
    loop(0, live, lambda slot: bring(slot).start())

    def clear(x):
        blank[x] = jnp.zeros(blank.shape[1:], jnp.bfloat16)

    loop(0, NX, clear)

    def wipe(core, quarter):
        return pltpu.make_async_copy(blank, share.at[core, quarter], sb.at[core, quarter])

    for core in range(2):
        for quarter in range(4):
            wipe(core, quarter).start()
    sketch[...] = jnp.zeros_like(sketch)

    def unseen(step):
        for u in range(8):
            seen[step * 8 + u] = -1

    loop(0, seen.shape[0] // 8, unseen)

    def number(slot):
        first[slot] = slot

    loop(0, first.shape[0], number)

    def look(slot):
        before = seen[columns[slot]]
        chosen = jnp.where(before < 0, slot, before)
        seen[columns[slot]] = chosen
        first[slot] = chosen

    loop(0, live, look)
    loop(0, live, lambda slot: bring(slot).wait())
    bring_values.wait()

    def add_sketch(step):
        products = []
        for u in range(UNROLL):
            slot = step * UNROLL + u
            picked = omega[slot].reshape(BLOCK, omega.shape[-1])
            products.append(jnp.dot(values[slot], picked, preferred_element_type=jnp.float32))
        for u in range(UNROLL):
            slot = step * UNROLL + u
            row = rows[slot] % RB_DEV
            sketch[row] = sketch[row] + jnp.where(slot < live, products[u], 0.0)

    loop(0, steps, add_sketch)
    gram[...] = jnp.zeros_like(gram)

    def add_gram(step):
        total = gram[...]
        for u in range(UNROLL):
            part = sketch[step * UNROLL + u]
            rounded[step * UNROLL + u] = part.astype(jnp.bfloat16)
            total = total + lax.dot_general(
                part, part, (((0,), (0,)), ((), ())), precision=precise, preferred_element_type=jnp.float32
            )
        gram[...] = total

    loop(0, sketch.shape[0] // UNROLL, add_gram)

    def add_share(step):
        products = []
        for u in range(UNROLL):
            slot = step * UNROLL + u
            products.append(
                lax.dot_general(
                    values[slot],
                    rounded[rows[slot] % RB_DEV],
                    (((0,), (0,)), ((), ())),
                    preferred_element_type=jnp.float32,
                )
            )
        for u in range(UNROLL):
            slot = step * UNROLL + u
            target = first[slot]
            totals[target] = jnp.where(target == slot, 0.0, totals[target]) + products[u]

    loop(0, steps, add_share)
    for core in range(2):
        for quarter in range(4):
            wipe(core, quarter).wait()

    def hand_out(slot):
        core, x, y, z = column_place(columns[slot])
        return pltpu.make_async_copy(packed.at[slot], share.at[core, :, x, y, z], sw.at[slot])

    def pack(step):
        for u in range(UNROLL):
            slot = step * UNROLL + u
            packed[slot] = totals[slot].astype(jnp.bfloat16).reshape(packed.shape[1:])
        for u in range(UNROLL):
            slot = step * UNROLL + u

            @pl.when((first[slot] == slot) & (slot < live))
            def _():
                hand_out(slot).start()

    loop(0, steps, pack)

    def done(slot):
        @pl.when(first[slot] == slot)
        def _():
            hand_out(slot).wait()

    loop(0, live, done)


def slab_products(values, columns, rows, count, omega):
    slots = values.shape[0]
    width = omega.shape[-1]
    smem = pl.BlockSpec(memory_space=pltpu.SMEM)
    vmem = pl.BlockSpec(memory_space=pltpu.VMEM)
    hbm = pl.BlockSpec(memory_space=pl.ANY)
    dma = pltpu.SemaphoreType.DMA
    f32, bf16 = jnp.float32, jnp.bfloat16
    return pl.pallas_call(
        slab_kernel,
        out_shape=(
            jax.ShapeDtypeStruct((RB_DEV, BLOCK, width), f32),
            jax.ShapeDtypeStruct((width, width), f32),
            jax.ShapeDtypeStruct((2, 4, NX, NY, NZ, QUARTER, width), bf16),
        ),
        in_specs=[smem, smem, smem, hbm, hbm],
        out_specs=(vmem, vmem, hbm),
        scratch_shapes=[
            pltpu.VMEM(values.shape, bf16),
            pltpu.VMEM((slots, 4, QUARTER, width), bf16),
            pltpu.VMEM((NX, NY, NZ, QUARTER, width), bf16),
            pltpu.VMEM((slots, BLOCK, width), f32),
            pltpu.VMEM((slots, 4, QUARTER, width), bf16),
            pltpu.VMEM((RB_DEV, BLOCK, width), bf16),
            pltpu.SMEM((NCOL // BLOCK,), jnp.int32),
            pltpu.SMEM((slots,), jnp.int32),
            dma,
            dma((slots,)),
            dma((2, 4)),
            dma((slots,)),
        ],
        compiler_params=pltpu.CompilerParams(vmem_limit_bytes=VMEM_LIMIT),
        name="slab_products",
    )(columns, rows, count, values, omega)


def project_kernel(columns, rows, count, values, basis, out, total):
    live = count[0]

    def clear(step):
        for core in range(2):
            for quarter in range(4):
                total[core, quarter, step // NY, step % NY] = jnp.zeros(total.shape[4:], jnp.float32)

    loop(0, NX * NY, clear)

    def some(step):
        for u in range(UNROLL):
            slot = step * UNROLL + u
            core, x, y, z = column_place(columns[slot])
            product = lax.dot_general(
                values[slot], basis[rows[slot] % RB_DEV], (((0,), (0,)), ((), ())), preferred_element_type=jnp.float32
            )
            product = jnp.where(slot < live, product, 0.0)
            for quarter in range(4):
                piece = product[quarter * QUARTER : (quarter + 1) * QUARTER]
                total[core, quarter, x, y, z] = total[core, quarter, x, y, z] + piece

    loop(0, (live + UNROLL - 1) // UNROLL, some)

    def narrow(step):
        x, y = step // NY, step % NY
        for core in range(2):
            for quarter in range(4):
                out[core, quarter, x, y] = total[core, quarter, x, y].astype(jnp.bfloat16)

    loop(0, NX * NY, narrow)


def project_slab(values, columns, rows, count, basis):
    width = basis.shape[-1]
    smem = pl.BlockSpec(memory_space=pltpu.SMEM)
    vmem = pl.BlockSpec(memory_space=pltpu.VMEM)
    shape = (2, 4, NX, NY, NZ, QUARTER, width)
    return pl.pallas_call(
        project_kernel,
        out_shape=jax.ShapeDtypeStruct(shape, jnp.bfloat16),
        in_specs=[smem, smem, smem, vmem, vmem],
        out_specs=vmem,
        scratch_shapes=[pltpu.VMEM(shape, jnp.float32)],
        compiler_params=pltpu.CompilerParams(vmem_limit_bytes=VMEM_LIMIT),
        name="project_slab",
    )(columns, rows, count, values, basis)


GROUP = 8


def factor_kernel(gram, upper, inverse, growth):
    size = gram.shape[0]
    tiles = size // 8
    lane = lax.broadcasted_iota(jnp.int32, (8, size), 1)
    sub = lax.broadcasted_iota(jnp.int32, (8, size), 0)
    left = [gram[8 * t : 8 * t + 8, :] for t in range(tiles)]
    right = [jnp.where(lane == sub + 8 * t, 1.0, 0.0).astype(jnp.float32) for t in range(tiles)]
    squares = jnp.zeros((8, size), jnp.float32)
    for t in range(tiles):
        squares = squares + jnp.where(lane == sub + 8 * t, left[t], 0.0)
    squares = jnp.sum(squares, axis=0, keepdims=True)
    for first in range(0, size, GROUP):
        home, base = first // 8, first % 8
        cols = [
            [jnp.broadcast_to(left[t][:, first + k : first + k + 1], (8, size)) for t in range(home, tiles)]
            for k in range(GROUP)
        ]
        pivot = [[cols[m][0][base + k : base + k + 1, :] for m in range(GROUP)] for k in range(GROUP)]
        row_left = [left[home][base + k : base + k + 1, :] for k in range(GROUP)]
        row_right = [right[home][base + k : base + k + 1, :] for k in range(GROUP)]
        for k in range(GROUP):
            over = 1.0 / pivot[k][k]
            for m in range(k + 1, GROUP):
                factor = pivot[k][m] * over
                for n in range(m, GROUP):
                    pivot[m][n] = pivot[m][n] - factor * pivot[k][n]
                row_left[m] = row_left[m] - factor * row_left[k]
                row_right[m] = row_right[m] - factor * row_right[k]
                cols[m] = [c - b * factor for c, b in zip(cols[m], cols[k])]
            row_left[k] = row_left[k] * over
            row_right[k] = row_right[k] * over
        for k in range(GROUP):
            cols[k][0] = jnp.where(sub > base + k, cols[k][0], 0.0)
        for t in range(home, tiles):
            for k in range(GROUP):
                left[t] = left[t] - cols[k][t - home] * row_left[k]
                right[t] = right[t] - cols[k][t - home] * row_right[k]
    spread = jnp.zeros((8, size), jnp.float32)
    for t in range(tiles):
        diagonal = jnp.sum(jnp.where(lane == sub + 8 * t, left[t], 0.0), axis=1, keepdims=True)
        over = 1.0 / jnp.sqrt(diagonal)
        upper[8 * t : 8 * t + 8, :] = jnp.where(lane >= sub + 8 * t, left[t] * over, 0.0)
        row = right[t] * over
        inverse[8 * t : 8 * t + 8, :] = row
        spread = spread + row * row * squares
    growth[0, 0] = jnp.sum(spread) * (1.0 / size)


def factor(gram):
    shape = jax.ShapeDtypeStruct(gram.shape, jnp.float32)
    vmem = pl.BlockSpec(memory_space=pltpu.VMEM)
    return pl.pallas_call(
        factor_kernel,
        out_shape=(shape, shape, jax.ShapeDtypeStruct((1, 1), jnp.float32)),
        in_specs=[vmem],
        out_specs=(vmem, vmem, pl.BlockSpec(memory_space=pltpu.SMEM)),
        name="factor",
    )(gram)


def full_dot(left, right, contract):
    return lax.dot_general(
        left, right, ((contract[:1], contract[1:]), ((), ())), precision=precise, preferred_element_type=jnp.float32
    )


def right_divide(row_block, lower_part):
    return lax.linalg.triangular_solve(
        lower_part, row_block, left_side=False, lower=True, transpose_a=True
    )


GROWTH_LIMIT = 2.0


def on_device(block_values, block_rows, block_cols, block_count, test_matrix):
    slot_count, width_block, _ = block_values.shape
    sketch_width = test_matrix.shape[1]
    slab_total = lax.axis_size("wide") * lax.axis_size("narrow")
    omega = gather_rows(test_matrix)
    sketch, gram, share = slab_products(block_values, block_cols, block_rows, block_count, omega)
    sketch = sketch.reshape(RB_DEV * width_block, sketch_width)
    total_rows = sketch.shape[0] * slab_total
    row_scale = math.sqrt(total_rows)
    column_scale = math.sqrt(NCOL / (slot_count * slab_total * width_block))
    summed, whole = scatter_shares(share, gram, 1)
    upper, inverse, growth = factor(whole)

    def one_pass(sketch, summed, whole, upper, inverse):
        q_basis = (full_dot(sketch, inverse, (1, 1)) * row_scale).astype(jnp.bfloat16)
        projected = full_dot(summed, inverse, (1, 1)) * (row_scale * column_scale)
        return q_basis, upper / row_scale, projected

    def two_passes(sketch, summed, whole, upper, inverse):
        lower_one = jnp.linalg.cholesky(whole)
        first_basis = right_divide(sketch, lower_one)
        second_gram = full_dot(first_basis, first_basis, (0, 0))
        lower_two = jnp.linalg.cholesky(total_over_devices(second_gram, 2))
        q_basis = (right_divide(first_basis, lower_two) * row_scale).astype(jnp.bfloat16)
        r_factor = full_dot(lower_one, lower_two, (1, 0)).T / row_scale
        basis_blocks = q_basis.reshape(RB_DEV, width_block, sketch_width)
        basis_share = project_slab(block_values, block_cols, block_rows, block_count, basis_blocks)
        projected, _ = scatter_shares(basis_share, second_gram, 3)
        return q_basis, r_factor, projected * column_scale

    return lax.cond(
        growth[0, 0] <= GROWTH_LIMIT, one_pass, two_passes, sketch, summed, whole, upper, inverse
    )


def solution(mesh):
    placed = (
        P(AXES, None, None),
        P(AXES),
        P(AXES),
        P(AXES),
        P(AXES, None),
    )
    return jax.shard_map(
        on_device,
        mesh=mesh,
        in_specs=placed,
        out_specs=(P(AXES, None), P(), P(AXES, None)),
        check_vma=False,
    )
```

```python
import math

import jax
import jax.numpy as jnp
from jax import lax
from jax.experimental import pallas as pl
from jax.experimental.pallas import tpu as pltpu
from jax.sharding import PartitionSpec as P

NCOL = 32768
RB_DEV = 16
BLOCK = 128
QUARTER = 32
NX, NY, NZ = 4, 4, 8

MESH = pl.DeviceIdType.MESH
AXES = ("wide", "narrow")
VMEM_LIMIT = 52 * 1024 * 1024

precise = lax.Precision.HIGHEST


def place():
    wide = lax.axis_index("wide")
    narrow = lax.axis_index("narrow")
    return narrow // NY, narrow % NY, wide // 2, wide % 2


def at(x, y, z, core):
    return (z * 2 + core, x * NY + y)


def column_place(column):
    narrow = column % (NX * NY)
    wide = column // (NX * NY)
    return wide % 2, narrow // NY, narrow % NY, wide // 2


def loop(low, high, body):
    def step(index, carry):
        body(index)
        return carry

    lax.fori_loop(low, high, step, 0)


def greet_torus(x, y, z, core):
    barrier = pltpu.get_barrier_semaphore()

    def greet(device):
        pl.semaphore_signal(barrier, inc=1, device_id=device, device_id_type=MESH)

    loop(1, NX, lambda k: greet(at((x + k) % NX, y, z, core)))
    loop(1, NY, lambda k: greet(at(x, (y + k) % NY, z, core)))
    loop(1, NZ, lambda k: greet(at(x, y, (z + k) % NZ, core)))
    greet(at(x, y, z, 1 - core))
    pl.semaphore_wait(barrier, NX + NY + NZ - 2)


def remote(src, dst, send, recv, device):
    return pltpu.make_async_remote_copy(
        src_ref=src, dst_ref=dst, send_sem=send, recv_sem=recv, device_id=device, device_id_type=MESH
    )


def gather_kernel(mine, out, local_sem, sz, rz, sa, ra, sn, rn, sf, rf, sc, rc):
    x, y, z, core = place()
    greet_torus(x, y, z, core)
    keep = pltpu.make_async_copy(mine, out.at[core, :, x, y, z], local_sem)

    def along(kind, step):
        if kind == 0:
            return at((x + step) % NX, y, z, core)
        return at(x, (y + step) % NY, z, core)

    def along_z(duo, k):
        source = mine.at[pl.ds(2 * duo, 2)]
        target = out.at[core, pl.ds(2 * duo, 2), x, y, z]
        return remote(source, target, sz.at[duo, k], rz.at[duo, k], at(x, y, (z + k) % NZ, core))

    def first(kind, duo, k):
        part = out.at[core, 2 * duo + kind, x, y]
        return remote(part, part, sa.at[kind, duo, k], ra.at[kind, duo, k], along(kind, k))

    def piece(kind, duo, back, half):
        if kind == 0:
            return out.at[core, 2 * duo, pl.ds(2 * half, 2), (y + NY - back) % NY]
        return out.at[core, 2 * duo + 1, (x + NX - back) % NX, pl.ds(2 * half, 2)]

    def near(kind, duo, side, half):
        part = piece(kind, duo, 0, half)
        send, recv = sn.at[kind, duo, side, half], rn.at[kind, duo, side, half]
        return remote(part, part, send, recv, along(1 - kind, 3 if side else 1))

    def far(kind, duo, side):
        back = 3 if side else 1
        part = piece(kind, duo, back, side)
        return remote(part, part, sf.at[kind, duo, side], rf.at[kind, duo, side], along(1 - kind, back))

    def across(kind, duo, back, half):
        part = piece(kind, duo, back, half)
        send, recv = sc.at[kind, duo, back, half], rc.at[kind, duo, back, half]
        return remote(part, part, send, recv, at(x, y, z, 1 - core))

    def start_first(duo):
        loop(1, NZ, lambda k: along_z(duo, k).wait_recv())
        for k in range(1, 4):
            for kind in range(2):
                first(kind, duo, k).start()

    def start_near(duo):
        for kind in range(2):
            loop(1, 4, lambda k: first(kind, duo, k).wait_recv())
            for turn in range(2):
                near(kind, duo, 0, turn).start()
                near(kind, duo, 1, 1 - turn).start()
        for kind in range(2):
            for half in range(2):
                across(kind, duo, 0, half).start()

    def start_far(duo):
        for kind in range(2):
            for side in range(2):
                near(kind, duo, side, side).wait_recv()
                far(kind, duo, side).start()
                across(kind, duo, 3 if side else 1, side).start()

    def pass_near(duo):
        for kind in range(2):
            for side in range(2):
                near(kind, duo, side, 1 - side).wait_recv()
                across(kind, duo, 3 if side else 1, 1 - side).start()

    def pass_far(duo):
        for kind in range(2):
            for side in range(2):
                far(kind, duo, side).wait_recv()
                across(kind, duo, 2, side).start()

    def drain_early(duo):
        loop(1, NZ, lambda k: along_z(duo, k).wait_send())
        for kind in range(2):
            loop(1, 4, lambda k: first(kind, duo, k).wait_send())

    def drain(duo):
        for kind in range(2):
            for side in range(2):
                for half in range(2):
                    near(kind, duo, side, half).wait_send()
                far(kind, duo, side).wait_send()
            for back in range(4):
                for half in range(2):
                    across(kind, duo, back, half).wait()

    loop(1, NZ, lambda k: along_z(0, k).start())
    keep.start()
    loop(1, NZ, lambda k: along_z(1, k).start())
    keep.wait()
    loop(0, 2, start_first)
    loop(0, 2, start_near)
    start_far(0)
    pass_near(0)
    start_far(1)
    pass_near(1)
    loop(0, 2, drain_early)
    loop(0, 2, pass_far)
    loop(0, 2, drain)


def gather_rows(test_matrix):
    width = test_matrix.shape[1]
    dma = pltpu.SemaphoreType.DMA
    return pl.pallas_call(
        gather_kernel,
        out_shape=jax.ShapeDtypeStruct((2, 4, NX, NY, NZ, QUARTER, width), jnp.bfloat16),
        in_specs=[pl.BlockSpec(memory_space=pl.ANY)],
        out_specs=pl.BlockSpec(memory_space=pl.ANY),
        scratch_shapes=[
            dma,
            dma((2, NZ)),
            dma((2, NZ)),
            dma((2, 2, 4)),
            dma((2, 2, 4)),
            dma((2, 2, 2, 2)),
            dma((2, 2, 2, 2)),
            dma((2, 2, 2)),
            dma((2, 2, 2)),
            dma((2, 2, 4, 2)),
            dma((2, 2, 4, 2)),
        ],
        compiler_params=pltpu.CompilerParams(collective_id=0, has_side_effects=True),
        name="gather_rows",
    )(test_matrix.reshape(4, QUARTER, width))


class gram_steps:
    def __init__(self, part, out, got, mid, got_z, both, s1, r1, s2, r2, s3, r3, sp, rp):
        self.part, self.out, self.got, self.mid, self.got_z, self.both = part, out, got, mid, got_z, both
        self.s1, self.r1, self.s2, self.r2, self.s3, self.r3 = s1, r1, s2, r2, s3, r3
        self.sp, self.rp = sp, rp
        self.wide, self.narrow = lax.axis_index("wide"), lax.axis_index("narrow")
        self.x, self.y, self.z, self.core = place()
        self.narrows = NX * NY
        self.rows = part.shape[0] // self.narrows

    def level(self, z, core):
        return at(self.x, self.y, z, core)

    def greet(self):
        barrier = pltpu.get_barrier_semaphore()

        def one(device):
            pl.semaphore_signal(barrier, inc=1, device_id=device, device_id_type=MESH)

        loop(1, NZ, lambda k: one(self.level((self.z + k) % NZ, self.core)))
        loop(1, self.narrows, lambda k: one((self.wide, (self.narrow + k) % self.narrows)))
        one(self.level(self.z, 1 - self.core))
        pl.semaphore_wait(barrier, self.narrows + NZ - 1)

    def chunk(self, ref, index):
        return ref.at[pl.ds(pl.multiple_of(index * self.rows, self.rows), self.rows)]

    def scatter(self, k):
        peer = (self.narrow + k) % self.narrows
        source = self.chunk(self.part, peer)
        return remote(source, self.got.at[self.narrow], self.s1.at[k], self.r1.at[k], (self.wide, peer))

    def exchange(self, k):
        device = self.level((self.z + k) % NZ, self.core)
        return remote(self.mid, self.got_z.at[self.z], self.s2.at[k], self.r2.at[k], device)

    def across(self):
        source = self.both.at[self.core]
        return remote(source, source, self.sp, self.rp, self.level(self.z, 1 - self.core))

    def spread(self, k):
        piece = self.chunk(self.out, self.narrow)
        device = (self.wide, (self.narrow + k) % self.narrows)
        return remote(piece, piece, self.s3.at[k], self.r3.at[k], device)

    def scatter_start(self):
        loop(1, self.narrows, lambda k: self.scatter(k).start())
        self.got[self.narrow] = self.chunk(self.part, self.narrow)[...]

    def scatter_finish(self):
        loop(1, self.narrows, lambda k: self.scatter(k).wait_recv())
        total = self.got[0]
        for index in range(1, self.narrows):
            total = total + self.got[index]
        self.mid[...] = total
        self.got_z[self.z] = total
        loop(1, NZ, lambda k: self.exchange(k).start())

    def exchange_finish(self):
        loop(1, NZ, lambda k: self.exchange(k).wait_recv())
        total = self.got_z[0]
        for index in range(1, NZ):
            total = total + self.got_z[index]
        self.both[self.core] = total
        self.across().start()

    def across_finish(self):
        self.across().wait()
        self.chunk(self.out, self.narrow)[...] = self.both[0] + self.both[1]
        loop(1, self.narrows, lambda k: self.spread(k).start())

    def drain_early(self):
        loop(1, self.narrows, lambda k: self.scatter(k).wait_send())
        loop(1, NZ, lambda k: self.exchange(k).wait_send())

    def spread_finish(self):
        loop(1, self.narrows, lambda k: self.spread(k).wait())


def total_kernel(part, out, *scratch):
    gram = gram_steps(part, out, *scratch)
    gram.greet()
    gram.scatter_start()
    gram.scatter_finish()
    gram.exchange_finish()
    gram.across_finish()
    gram.drain_early()
    gram.spread_finish()


def gram_buffers(matrix):
    narrows = NX * NY
    rows, width = matrix.shape[0] // narrows, matrix.shape[1]
    return [pltpu.VMEM((*count, rows, width), jnp.float32) for count in ((narrows,), (), (NZ,), (2,))]


def gram_semaphores():
    dma = pltpu.SemaphoreType.DMA
    return [dma((count,)) for count in (NX * NY, NX * NY, NZ, NZ, NX * NY, NX * NY)] + [dma, dma]


def total_over_devices(matrix, collective_id):
    return pl.pallas_call(
        total_kernel,
        out_shape=jax.ShapeDtypeStruct(matrix.shape, jnp.float32),
        in_specs=[pl.BlockSpec(memory_space=pltpu.VMEM)],
        out_specs=pl.BlockSpec(memory_space=pltpu.VMEM),
        scratch_shapes=gram_buffers(matrix) + gram_semaphores(),
        compiler_params=pltpu.CompilerParams(collective_id=collective_id, has_side_effects=True),
        name="total_gram",
    )(matrix)


GROUP = 4


def factor_into(gram, upper, inverse, growth):
    size = gram.shape[0]
    f32 = jnp.float32
    left = gram[...]
    lanes = lax.broadcasted_iota(jnp.int32, (size, size), 1)
    subs = lax.broadcasted_iota(jnp.int32, (size, size), 0)
    right = jnp.where(lanes == subs, 1.0, 0.0).astype(f32)
    squares = jnp.sum(jnp.where(lanes == subs, left, 0.0), axis=0, keepdims=True)
    spread = jnp.zeros((8, size), f32)
    for first in range(0, size, GROUP):
        base = first % 8
        cols = [jnp.broadcast_to(left[:, first + k : first + k + 1], left.shape) for k in range(GROUP)]
        pivot = [[cols[m][base + k : base + k + 1, :] for m in range(GROUP)] for k in range(GROUP)]
        row_left = [left[base + k : base + k + 1, :] for k in range(GROUP)]
        row_right = [right[base + k : base + k + 1, :] for k in range(GROUP)]
        for k in range(GROUP):
            over = 1.0 / pivot[k][k]
            for m in range(k + 1, GROUP):
                factor = pivot[k][m] * over
                for n in range(m, GROUP):
                    pivot[m][n] = pivot[m][n] - factor * pivot[k][n]
                row_left[m] = row_left[m] - factor * row_left[k]
                row_right[m] = row_right[m] - factor * row_right[k]
                cols[m] = cols[m] - cols[k] * factor
            row_left[k] = row_left[k] * over
            row_right[k] = row_right[k] * over
        index = subs[: left.shape[0]]
        for k in range(GROUP):
            below = jnp.where(index > base + k, cols[k], 0.0)
            left = left - below * row_left[k]
            right = right - below * row_right[k]
        if base + GROUP == 8:
            top = first + GROUP - 8
            lane, sub = lanes[:8], subs[:8] + top
            diagonal = jnp.sum(jnp.where(lane == sub, left[:8], 0.0), axis=1, keepdims=True)
            over = 1.0 / jnp.sqrt(diagonal)
            upper[top : top + 8, :] = jnp.where(lane >= sub, left[:8] * over, 0.0)
            row = right[:8] * over
            inverse[top : top + 8, :] = row
            spread = spread + row * row * squares
            left, right = left[8:], right[8:]
    growth[0, 0] = jnp.sum(spread) * (1.0 / size)


def scatter_kernel(
    share, part, out, whole, upper, inverse, growth, own, got, far_in, near_in, pair, cross_in, last, z_in, got_narrow, mid, got_z, both,
    so, sc, rc, sf, rf, sn, rn, sb, rb, sz, rz, *gram_sems,
):
    x, y, z, core = place()
    other = 1 - core
    f32, bf16 = jnp.float32, jnp.bfloat16
    gram = gram_steps(part, whole, got_narrow, mid, got_z, both, *gram_sems)

    def along(kind, step):
        if kind == 0:
            return at((x + step) % NX, y, z, core)
        return at(x, (y + step) % NY, z, core)

    def chunk(ref, kind, duo, step):
        if kind == 0:
            return ref.at[2 * duo, (x + step) % NX]
        return ref.at[2 * duo + 1, :, (y + step) % NY]

    def half_of(ref, kind, duo, step, half):
        if kind == 0:
            return ref.at[2 * duo, (x + step) % NX, pl.ds(2 * half, 2)]
        return ref.at[2 * duo + 1, pl.ds(2 * half, 2), (y + step) % NY]

    def line(ref, kind, duo, step, index):
        if kind == 0:
            return ref.at[2 * duo, (x + step) % NX, index]
        return ref.at[2 * duo + 1, index, (y + step) % NY]

    mine = pltpu.make_async_copy(share.at[core], own, so)

    def across(kind, duo, step):
        source, target = chunk(share.at[other], kind, duo, step), chunk(got, kind, duo, step)
        return remote(source, target, sc.at[kind, duo, step], rc.at[kind, duo, step], at(x, y, z, other))

    def far(kind, duo, side):
        source = half_of(own, kind, duo, 2, side)
        return remote(
            source, far_in.at[kind, duo, side], sf.at[kind, duo, side], rf.at[kind, duo, side],
            along(kind, 3 if side else 1),
        )

    def near(kind, duo, side, half):
        step = 3 if side else 1
        source = half_of(own, kind, duo, step, half)
        target = near_in.at[kind, duo, side, pl.ds(2 * half, 2)]
        return remote(
            source, target, sn.at[kind, duo, side, half], rn.at[kind, duo, side, half], along(kind, step)
        )

    def cross(kind, duo, k):
        to = (y + k) % NY if kind == 0 else (x + k) % NX
        return remote(
            pair.at[kind, duo, to], cross_in.at[kind, duo, k - 1], sb.at[kind, duo, k], rb.at[kind, duo, k],
            along(1 - kind, k),
        )

    def third(duo, k):
        to = (z + k) % NZ
        return remote(
            last.at[duo, to], z_in.at[duo, k - 1], sz.at[duo, k], rz.at[duo, k], at(x, y, to, core)
        )

    order = (2, 1, 3, 0)

    def send_over(duo):
        for step in order:
            for kind in range(2):
                across(kind, duo, step).start()

    def join(kind, duo, step):
        across(kind, duo, step).wait_recv()

        def add(index):
            a, b = line(own, kind, duo, step, index), line(got, kind, duo, step, index)
            a[...] = (a[...].astype(f32) + b[...].astype(f32)).astype(bf16)

        loop(0, 4, add)

    def first_far(duo):
        for kind in range(2):
            join(kind, duo, 2)
            far(kind, duo, 0).start()
            far(kind, duo, 1).start()

    def first_near(duo):
        for kind in range(2):
            for side in range(2):
                join(kind, duo, 3 if side else 1)
                near(kind, duo, side, 1 - side).start()
        for kind in range(2):
            for side in range(2):
                far(kind, duo, side).wait_recv()

                def add(index):
                    a = line(own, kind, duo, 3 if side else 1, 2 * side + index)
                    a[...] = (a[...].astype(f32) + far_in[kind, duo, side, index].astype(f32)).astype(bf16)

                loop(0, 2, add)
                near(kind, duo, side, side).start()
        for kind in range(2):
            join(kind, duo, 0)

    def second(duo):
        for kind in range(2):
            for side in range(2):
                for half in range(2):
                    near(kind, duo, side, half).wait_recv()

            def add(index):
                total = line(own, kind, duo, 0, index)[...].astype(f32)
                total = total + near_in[kind, duo, 0, index].astype(f32)
                total = total + near_in[kind, duo, 1, index].astype(f32)
                pair[kind, duo, index] = total.astype(bf16)

            loop(0, 4, add)
            loop(1, 4, lambda k: cross(kind, duo, k).start())

    def final(duo):
        for kind in range(2):
            loop(1, 4, lambda k: cross(kind, duo, k).wait_recv())

        def add(k):
            index = (z + k) % NZ
            for kind in range(2):
                total = pair[kind, duo, y if kind == 0 else x, index].astype(f32)
                for j in range(3):
                    total = total + cross_in[kind, duo, j, index].astype(f32)
                last[duo, index, kind] = total.astype(bf16)

        def send(k):
            add(k)
            third(duo, k).start()

        loop(0, 3, lambda k: send(4 - k))
        loop(5, NZ, send)
        send(1)
        add(0)

    def finish(duo):
        loop(1, NZ, lambda k: third(duo, k).wait_recv())
        total = last[duo, z].astype(f32)
        for k in range(NZ - 1):
            total = total + z_in[duo, k].astype(f32)
        out[duo] = total

    def drain_first(duo):
        for kind in range(2):
            loop(0, 4, lambda step: across(kind, duo, step).wait_send())
            for side in range(2):
                far(kind, duo, side).wait_send()

    def drain_second(duo):
        for kind in range(2):
            for side in range(2):
                for half in range(2):
                    near(kind, duo, side, half).wait_send()
            loop(1, 4, lambda k: cross(kind, duo, k).wait_send())

    mine.start()
    gram.greet()
    loop(0, 2, send_over)
    mine.wait()
    first_far(0)
    gram.scatter_start()
    first_near(0)
    first_far(1)
    first_near(1)
    gram.scatter_finish()
    gram.exchange_finish()
    second(0)
    gram.across_finish()
    second(1)
    loop(0, 2, drain_first)
    gram.drain_early()
    loop(0, 2, final)
    loop(0, 2, drain_second)
    gram.spread_finish()
    factor_into(whole, upper, inverse, growth)
    loop(0, 2, finish)
    loop(0, 2, lambda duo: loop(1, NZ, lambda k: third(duo, k).wait_send()))


def scatter_shares(share, gram, collective_id):
    width = share.shape[-1]
    bf16 = jnp.bfloat16
    dma = pltpu.SemaphoreType.DMA
    tail = (NZ, QUARTER, width)
    vmem = pltpu.VMEM
    in_vmem = pl.BlockSpec(memory_space=pltpu.VMEM)
    square = jax.ShapeDtypeStruct(gram.shape, jnp.float32)
    summed, *factored = pl.pallas_call(
        scatter_kernel,
        out_shape=(
            jax.ShapeDtypeStruct((2, 2, QUARTER, width), jnp.float32),
            square,
            square,
            square,
            jax.ShapeDtypeStruct((1, 1), jnp.float32),
        ),
        in_specs=[pl.BlockSpec(memory_space=pl.ANY), in_vmem],
        out_specs=(in_vmem, in_vmem, in_vmem, in_vmem, pl.BlockSpec(memory_space=pltpu.SMEM)),
        scratch_shapes=[
            vmem((4, NX, NY, *tail), bf16),
            vmem((4, NX, NY, *tail), bf16),
            vmem((2, 2, 2, 2, *tail), bf16),
            vmem((2, 2, 2, 4, *tail), bf16),
            vmem((2, 2, 4, *tail), bf16),
            vmem((2, 2, 3, *tail), bf16),
            vmem((2, NZ, 2, QUARTER, width), bf16),
            vmem((2, NZ - 1, 2, QUARTER, width), bf16),
            *gram_buffers(gram),
            dma,
            dma((2, 2, 4)),
            dma((2, 2, 4)),
            dma((2, 2, 2)),
            dma((2, 2, 2)),
            dma((2, 2, 2, 2)),
            dma((2, 2, 2, 2)),
            dma((2, 2, 4)),
            dma((2, 2, 4)),
            dma((2, NZ)),
            dma((2, NZ)),
            *gram_semaphores(),
        ],
        compiler_params=pltpu.CompilerParams(
            collective_id=collective_id, has_side_effects=True, vmem_limit_bytes=VMEM_LIMIT
        ),
        name="scatter_shares",
    )(share, gram)
    return summed.reshape(4 * QUARTER, width), *factored


UNROLL = 16


def slab_kernel(
    columns, rows, count, values_hbm, omega_hbm, sketch, gram, share,
    values, omega, blank, totals, packed, rounded, seen, first, sv, so, sb, sw,
):
    live = count[0]
    steps = (live + UNROLL - 1) // UNROLL
    bring_values = pltpu.make_async_copy(values_hbm, values, sv)

    def bring(slot):
        core, x, y, z = column_place(columns[slot])
        return pltpu.make_async_copy(omega_hbm.at[core, :, x, y, z], omega.at[slot], so.at[slot])

    bring_values.start()
    loop(0, live, lambda slot: bring(slot).start())

    def clear(x):
        blank[x] = jnp.zeros(blank.shape[1:], jnp.bfloat16)

    loop(0, NX, clear)

    def wipe(core, quarter):
        return pltpu.make_async_copy(blank, share.at[core, quarter], sb.at[core, quarter])

    for core in range(2):
        for quarter in range(4):
            wipe(core, quarter).start()
    sketch[...] = jnp.zeros_like(sketch)

    def unseen(step):
        for u in range(8):
            seen[step * 8 + u] = -1

    loop(0, seen.shape[0] // 8, unseen)

    def number(slot):
        first[slot] = slot

    loop(live, steps * UNROLL, number)

    def look(slot):
        before = seen[columns[slot]]
        chosen = jnp.where(before < 0, slot, before)
        seen[columns[slot]] = chosen
        first[slot] = chosen

    loop(0, live, look)
    loop(0, live, lambda slot: bring(slot).wait())
    bring_values.wait()

    def add_sketch(step):
        products = []
        for u in range(UNROLL):
            slot = step * UNROLL + u
            picked = omega[slot].reshape(BLOCK, omega.shape[-1])
            products.append(jnp.dot(values[slot], picked, preferred_element_type=jnp.float32))
        for u in range(UNROLL):
            slot = step * UNROLL + u
            row = rows[slot] % RB_DEV
            sketch[row] = sketch[row] + jnp.where(slot < live, products[u], 0.0)

    loop(0, steps, add_sketch)
    rounded[...] = sketch[...].astype(jnp.bfloat16)

    def add_share(step):
        products = []
        for u in range(UNROLL):
            slot = step * UNROLL + u
            products.append(
                lax.dot_general(
                    values[slot],
                    rounded[rows[slot] % RB_DEV],
                    (((0,), (0,)), ((), ())),
                    preferred_element_type=jnp.float32,
                )
            )
        for u in range(UNROLL):
            slot = step * UNROLL + u
            target = first[slot]
            totals[target] = jnp.where(target == slot, 0.0, totals[target]) + products[u]

    loop(0, steps, add_share)
    for core in range(2):
        for quarter in range(4):
            wipe(core, quarter).wait()

    def hand_out(slot):
        core, x, y, z = column_place(columns[slot])
        return pltpu.make_async_copy(packed.at[slot], share.at[core, :, x, y, z], sw.at[slot])

    def pack(step):
        for u in range(UNROLL):
            slot = step * UNROLL + u
            packed[slot] = totals[slot].astype(jnp.bfloat16).reshape(packed.shape[1:])
        for u in range(UNROLL):
            slot = step * UNROLL + u

            @pl.when((first[slot] == slot) & (slot < live))
            def _():
                hand_out(slot).start()

    loop(0, steps, pack)
    gram[...] = jnp.zeros_like(gram)

    def add_gram(step):
        total = gram[...]
        for u in range(UNROLL):
            part = sketch[step * UNROLL + u]
            total = total + lax.dot_general(
                part, part, (((0,), (0,)), ((), ())), precision=precise, preferred_element_type=jnp.float32
            )
        gram[...] = total

    loop(0, sketch.shape[0] // UNROLL, add_gram)

    def done(slot):
        @pl.when(first[slot] == slot)
        def _():
            hand_out(slot).wait()

    loop(0, live, done)


def slab_products(values, columns, rows, count, omega):
    slots = values.shape[0]
    width = omega.shape[-1]
    smem = pl.BlockSpec(memory_space=pltpu.SMEM)
    vmem = pl.BlockSpec(memory_space=pltpu.VMEM)
    hbm = pl.BlockSpec(memory_space=pl.ANY)
    dma = pltpu.SemaphoreType.DMA
    f32, bf16 = jnp.float32, jnp.bfloat16
    return pl.pallas_call(
        slab_kernel,
        out_shape=(
            jax.ShapeDtypeStruct((RB_DEV, BLOCK, width), f32),
            jax.ShapeDtypeStruct((width, width), f32),
            jax.ShapeDtypeStruct((2, 4, NX, NY, NZ, QUARTER, width), bf16),
        ),
        in_specs=[smem, smem, smem, hbm, hbm],
        out_specs=(vmem, vmem, hbm),
        scratch_shapes=[
            pltpu.VMEM(values.shape, bf16),
            pltpu.VMEM((slots, 4, QUARTER, width), bf16),
            pltpu.VMEM((NX, NY, NZ, QUARTER, width), bf16),
            pltpu.VMEM((slots, BLOCK, width), f32),
            pltpu.VMEM((slots, 4, QUARTER, width), bf16),
            pltpu.VMEM((RB_DEV, BLOCK, width), bf16),
            pltpu.SMEM((NCOL // BLOCK,), jnp.int32),
            pltpu.SMEM((slots,), jnp.int32),
            dma,
            dma((slots,)),
            dma((2, 4)),
            dma((slots,)),
        ],
        compiler_params=pltpu.CompilerParams(vmem_limit_bytes=VMEM_LIMIT),
        name="slab_products",
    )(columns, rows, count, values, omega)


def project_kernel(columns, rows, count, values, basis, out, total):
    live = count[0]

    def clear(step):
        for core in range(2):
            for quarter in range(4):
                total[core, quarter, step // NY, step % NY] = jnp.zeros(total.shape[4:], jnp.float32)

    loop(0, NX * NY, clear)

    def some(step):
        for u in range(UNROLL):
            slot = step * UNROLL + u
            core, x, y, z = column_place(columns[slot])
            product = lax.dot_general(
                values[slot], basis[rows[slot] % RB_DEV], (((0,), (0,)), ((), ())), preferred_element_type=jnp.float32
            )
            product = jnp.where(slot < live, product, 0.0)
            for quarter in range(4):
                piece = product[quarter * QUARTER : (quarter + 1) * QUARTER]
                total[core, quarter, x, y, z] = total[core, quarter, x, y, z] + piece

    loop(0, (live + UNROLL - 1) // UNROLL, some)

    def narrow(step):
        x, y = step // NY, step % NY
        for core in range(2):
            for quarter in range(4):
                out[core, quarter, x, y] = total[core, quarter, x, y].astype(jnp.bfloat16)

    loop(0, NX * NY, narrow)


def project_slab(values, columns, rows, count, basis):
    width = basis.shape[-1]
    smem = pl.BlockSpec(memory_space=pltpu.SMEM)
    vmem = pl.BlockSpec(memory_space=pltpu.VMEM)
    shape = (2, 4, NX, NY, NZ, QUARTER, width)
    return pl.pallas_call(
        project_kernel,
        out_shape=jax.ShapeDtypeStruct(shape, jnp.bfloat16),
        in_specs=[smem, smem, smem, vmem, vmem],
        out_specs=vmem,
        scratch_shapes=[pltpu.VMEM(shape, jnp.float32)],
        compiler_params=pltpu.CompilerParams(vmem_limit_bytes=VMEM_LIMIT),
        name="project_slab",
    )(columns, rows, count, values, basis)


def full_dot(left, right, contract):
    return lax.dot_general(
        left, right, ((contract[:1], contract[1:]), ((), ())), precision=precise, preferred_element_type=jnp.float32
    )


def right_divide(row_block, lower_part):
    return lax.linalg.triangular_solve(
        lower_part, row_block, left_side=False, lower=True, transpose_a=True
    )


GROWTH_LIMIT = 2.0


def on_device(block_values, block_rows, block_cols, block_count, test_matrix):
    slot_count, width_block, _ = block_values.shape
    sketch_width = test_matrix.shape[1]
    slab_total = lax.axis_size("wide") * lax.axis_size("narrow")
    omega = gather_rows(test_matrix)
    sketch, gram, share = slab_products(block_values, block_cols, block_rows, block_count, omega)
    sketch = sketch.reshape(RB_DEV * width_block, sketch_width)
    total_rows = sketch.shape[0] * slab_total
    row_scale = math.sqrt(total_rows)
    column_scale = math.sqrt(NCOL / (slot_count * slab_total * width_block))
    summed, whole, upper, inverse, growth = scatter_shares(share, gram, 1)

    def one_pass(sketch, summed, whole, upper, inverse):
        q_basis = (full_dot(sketch, inverse, (1, 1)) * row_scale).astype(jnp.bfloat16)
        projected = full_dot(summed, inverse, (1, 1)) * (row_scale * column_scale)
        return q_basis, upper / row_scale, projected

    def two_passes(sketch, summed, whole, upper, inverse):
        lower_one = jnp.linalg.cholesky(whole)
        first_basis = right_divide(sketch, lower_one)
        second_gram = full_dot(first_basis, first_basis, (0, 0))
        lower_two = jnp.linalg.cholesky(total_over_devices(second_gram, 2))
        q_basis = (right_divide(first_basis, lower_two) * row_scale).astype(jnp.bfloat16)
        r_factor = full_dot(lower_one, lower_two, (1, 0)).T / row_scale
        basis_blocks = q_basis.reshape(RB_DEV, width_block, sketch_width)
        basis_share = project_slab(block_values, block_cols, block_rows, block_count, basis_blocks)
        projected, *_ = scatter_shares(basis_share, second_gram, 3)
        return q_basis, r_factor, projected * column_scale

    return lax.cond(
        growth[0, 0] <= GROWTH_LIMIT, one_pass, two_passes, sketch, summed, whole, upper, inverse
    )


def solution(mesh):
    placed = (
        P(AXES, None, None),
        P(AXES),
        P(AXES),
        P(AXES),
        P(AXES, None),
    )
    return jax.shard_map(
        on_device,
        mesh=mesh,
        in_specs=placed,
        out_specs=(P(AXES, None), P(), P(AXES, None)),
        check_vma=False,
    )
```

```python
import math

import jax
import jax.numpy as jnp
from jax import lax
from jax.experimental import pallas as pl
from jax.experimental.pallas import tpu as pltpu
from jax.sharding import PartitionSpec as P

NCOL = 32768
RB_DEV = 16
BLOCK = 128
QUARTER = 32
NX, NY, NZ = 4, 4, 8

MESH = pl.DeviceIdType.MESH
AXES = ("wide", "narrow")
VMEM_LIMIT = 52 * 1024 * 1024

precise = lax.Precision.HIGHEST


def place():
    wide = lax.axis_index("wide")
    narrow = lax.axis_index("narrow")
    return narrow // NY, narrow % NY, wide // 2, wide % 2


def at(x, y, z, core):
    return (z * 2 + core, x * NY + y)


def column_place(column):
    narrow = column % (NX * NY)
    wide = column // (NX * NY)
    return wide % 2, narrow // NY, narrow % NY, wide // 2


def loop(low, high, body):
    def step(index, carry):
        body(index)
        return carry

    lax.fori_loop(low, high, step, 0)


def greet_torus(x, y, z, core):
    barrier = pltpu.get_barrier_semaphore()

    def greet(device):
        pl.semaphore_signal(barrier, inc=1, device_id=device, device_id_type=MESH)

    loop(1, NX, lambda k: greet(at((x + k) % NX, y, z, core)))
    loop(1, NY, lambda k: greet(at(x, (y + k) % NY, z, core)))
    loop(1, NZ, lambda k: greet(at(x, y, (z + k) % NZ, core)))
    greet(at(x, y, z, 1 - core))
    pl.semaphore_wait(barrier, NX + NY + NZ - 2)


def remote(src, dst, send, recv, device):
    return pltpu.make_async_remote_copy(
        src_ref=src, dst_ref=dst, send_sem=send, recv_sem=recv, device_id=device, device_id_type=MESH
    )


def gather_kernel(mine, out, local_sem, sz, rz, sa, ra, sn, rn, sf, rf, sc, rc):
    x, y, z, core = place()
    greet_torus(x, y, z, core)
    keep = pltpu.make_async_copy(mine, out.at[core, :, x, y, z], local_sem)

    def along(kind, step):
        if kind == 0:
            return at((x + step) % NX, y, z, core)
        return at(x, (y + step) % NY, z, core)

    def along_z(duo, k):
        source = mine.at[pl.ds(2 * duo, 2)]
        target = out.at[core, pl.ds(2 * duo, 2), x, y, z]
        return remote(source, target, sz.at[duo, k], rz.at[duo, k], at(x, y, (z + k) % NZ, core))

    def first(kind, duo, k):
        part = out.at[core, 2 * duo + kind, x, y]
        return remote(part, part, sa.at[kind, duo, k], ra.at[kind, duo, k], along(kind, k))

    def piece(kind, duo, back, half):
        if kind == 0:
            return out.at[core, 2 * duo, pl.ds(2 * half, 2), (y + NY - back) % NY]
        return out.at[core, 2 * duo + 1, (x + NX - back) % NX, pl.ds(2 * half, 2)]

    def near(kind, duo, side, half):
        part = piece(kind, duo, 0, half)
        send, recv = sn.at[kind, duo, side, half], rn.at[kind, duo, side, half]
        return remote(part, part, send, recv, along(1 - kind, 3 if side else 1))

    def far(kind, duo, side):
        back = 3 if side else 1
        part = piece(kind, duo, back, side)
        return remote(part, part, sf.at[kind, duo, side], rf.at[kind, duo, side], along(1 - kind, back))

    def across(kind, duo, back, half):
        part = piece(kind, duo, back, half)
        send, recv = sc.at[kind, duo, back, half], rc.at[kind, duo, back, half]
        return remote(part, part, send, recv, at(x, y, z, 1 - core))

    def start_first(duo):
        loop(1, NZ, lambda k: along_z(duo, k).wait_recv())
        for k in range(1, 4):
            for kind in range(2):
                first(kind, duo, k).start()

    def start_near(duo):
        for kind in range(2):
            loop(1, 4, lambda k: first(kind, duo, k).wait_recv())
            for turn in range(2):
                near(kind, duo, 0, turn).start()
                near(kind, duo, 1, 1 - turn).start()
        for kind in range(2):
            for half in range(2):
                across(kind, duo, 0, half).start()

    def start_far(duo):
        for kind in range(2):
            for side in range(2):
                near(kind, duo, side, side).wait_recv()
                far(kind, duo, side).start()
                across(kind, duo, 3 if side else 1, side).start()

    def pass_near(duo):
        for kind in range(2):
            for side in range(2):
                near(kind, duo, side, 1 - side).wait_recv()
                across(kind, duo, 3 if side else 1, 1 - side).start()

    def pass_far(duo):
        for kind in range(2):
            for side in range(2):
                far(kind, duo, side).wait_recv()
                across(kind, duo, 2, side).start()

    def drain_early(duo):
        loop(1, NZ, lambda k: along_z(duo, k).wait_send())
        for kind in range(2):
            loop(1, 4, lambda k: first(kind, duo, k).wait_send())

    def drain(duo):
        for kind in range(2):
            for side in range(2):
                for half in range(2):
                    near(kind, duo, side, half).wait_send()
                far(kind, duo, side).wait_send()
            for back in range(4):
                for half in range(2):
                    across(kind, duo, back, half).wait()

    loop(1, NZ, lambda k: along_z(0, k).start())
    keep.start()
    loop(1, NZ, lambda k: along_z(1, k).start())
    keep.wait()
    loop(0, 2, start_first)
    loop(0, 2, start_near)
    start_far(0)
    pass_near(0)
    start_far(1)
    pass_near(1)
    loop(0, 2, drain_early)
    loop(0, 2, pass_far)
    loop(0, 2, drain)


def gather_rows(test_matrix):
    width = test_matrix.shape[1]
    dma = pltpu.SemaphoreType.DMA
    return pl.pallas_call(
        gather_kernel,
        out_shape=jax.ShapeDtypeStruct((2, 4, NX, NY, NZ, QUARTER, width), jnp.bfloat16),
        in_specs=[pl.BlockSpec(memory_space=pl.ANY)],
        out_specs=pl.BlockSpec(memory_space=pl.ANY),
        scratch_shapes=[
            dma,
            dma((2, NZ)),
            dma((2, NZ)),
            dma((2, 2, 4)),
            dma((2, 2, 4)),
            dma((2, 2, 2, 2)),
            dma((2, 2, 2, 2)),
            dma((2, 2, 2)),
            dma((2, 2, 2)),
            dma((2, 2, 4, 2)),
            dma((2, 2, 4, 2)),
        ],
        compiler_params=pltpu.CompilerParams(collective_id=0, has_side_effects=True),
        name="gather_rows",
    )(test_matrix.reshape(4, QUARTER, width))


class gram_steps:
    def __init__(self, part, out, got, mid, got_z, both, s1, r1, s2, r2, s3, r3, sp, rp):
        self.part, self.out, self.got, self.mid, self.got_z, self.both = part, out, got, mid, got_z, both
        self.s1, self.r1, self.s2, self.r2, self.s3, self.r3 = s1, r1, s2, r2, s3, r3
        self.sp, self.rp = sp, rp
        self.wide, self.narrow = lax.axis_index("wide"), lax.axis_index("narrow")
        self.x, self.y, self.z, self.core = place()
        self.narrows = NX * NY
        self.rows = part.shape[0] // self.narrows

    def level(self, z, core):
        return at(self.x, self.y, z, core)

    def hail(self):
        barrier = pltpu.get_barrier_semaphore()

        def one(device):
            pl.semaphore_signal(barrier, inc=1, device_id=device, device_id_type=MESH)

        loop(1, NZ, lambda k: one(self.level((self.z + k) % NZ, self.core)))
        loop(1, self.narrows, lambda k: one((self.wide, (self.narrow + k) % self.narrows)))
        one(self.level(self.z, 1 - self.core))

    def greet(self):
        pl.semaphore_wait(pltpu.get_barrier_semaphore(), self.narrows + NZ - 1)

    def chunk(self, ref, index):
        return ref.at[pl.ds(pl.multiple_of(index * self.rows, self.rows), self.rows)]

    def scatter(self, k):
        peer = (self.narrow + k) % self.narrows
        source = self.chunk(self.part, peer)
        return remote(source, self.got.at[self.narrow], self.s1.at[k], self.r1.at[k], (self.wide, peer))

    def exchange(self, k):
        device = self.level((self.z + k) % NZ, self.core)
        return remote(self.mid, self.got_z.at[self.z], self.s2.at[k], self.r2.at[k], device)

    def across(self):
        source = self.both.at[self.core]
        return remote(source, source, self.sp, self.rp, self.level(self.z, 1 - self.core))

    def spread(self, k):
        piece = self.chunk(self.out, self.narrow)
        device = (self.wide, (self.narrow + k) % self.narrows)
        return remote(piece, piece, self.s3.at[k], self.r3.at[k], device)

    def scatter_start(self):
        loop(1, self.narrows, lambda k: self.scatter(k).start())
        self.got[self.narrow] = self.chunk(self.part, self.narrow)[...]

    def scatter_finish(self):
        loop(1, self.narrows, lambda k: self.scatter(k).wait_recv())
        total = self.got[0]
        for index in range(1, self.narrows):
            total = total + self.got[index]
        self.mid[...] = total
        self.got_z[self.z] = total
        loop(1, NZ, lambda k: self.exchange(k).start())

    def exchange_finish(self):
        loop(1, NZ, lambda k: self.exchange(k).wait_recv())
        total = self.got_z[0]
        for index in range(1, NZ):
            total = total + self.got_z[index]
        self.both[self.core] = total
        self.across().start()

    def across_finish(self):
        self.across().wait()
        self.chunk(self.out, self.narrow)[...] = self.both[0] + self.both[1]
        loop(1, self.narrows, lambda k: self.spread(k).start())

    def drain_early(self):
        loop(1, self.narrows, lambda k: self.scatter(k).wait_send())
        loop(1, NZ, lambda k: self.exchange(k).wait_send())

    def spread_finish(self):
        loop(1, self.narrows, lambda k: self.spread(k).wait())


def total_kernel(part, out, *scratch):
    gram = gram_steps(part, out, *scratch)
    gram.hail()
    gram.greet()
    gram.scatter_start()
    gram.scatter_finish()
    gram.exchange_finish()
    gram.across_finish()
    gram.drain_early()
    gram.spread_finish()


def gram_buffers(matrix):
    narrows = NX * NY
    rows, width = matrix.shape[0] // narrows, matrix.shape[1]
    return [pltpu.VMEM((*count, rows, width), jnp.float32) for count in ((narrows,), (), (NZ,), (2,))]


def gram_semaphores():
    dma = pltpu.SemaphoreType.DMA
    return [dma((count,)) for count in (NX * NY, NX * NY, NZ, NZ, NX * NY, NX * NY)] + [dma, dma]


def total_over_devices(matrix, collective_id):
    return pl.pallas_call(
        total_kernel,
        out_shape=jax.ShapeDtypeStruct(matrix.shape, jnp.float32),
        in_specs=[pl.BlockSpec(memory_space=pltpu.VMEM)],
        out_specs=pl.BlockSpec(memory_space=pltpu.VMEM),
        scratch_shapes=gram_buffers(matrix) + gram_semaphores(),
        compiler_params=pltpu.CompilerParams(collective_id=collective_id, has_side_effects=True),
        name="total_gram",
    )(matrix)


GROUP = 4


def factor_into(gram, upper, inverse, growth):
    size = gram.shape[0]
    f32 = jnp.float32
    left = gram[...]
    lanes = lax.broadcasted_iota(jnp.int32, (size, size), 1)
    subs = lax.broadcasted_iota(jnp.int32, (size, size), 0)
    right = jnp.where(lanes == subs, 1.0, 0.0).astype(f32)
    squares = jnp.sum(jnp.where(lanes == subs, left, 0.0), axis=0, keepdims=True)
    spread = jnp.zeros((8, size), f32)
    for first in range(0, size, GROUP):
        base = first % 8
        cols = [jnp.broadcast_to(left[:, first + k : first + k + 1], left.shape) for k in range(GROUP)]
        pivot = [[cols[m][base + k : base + k + 1, :] for m in range(GROUP)] for k in range(GROUP)]
        row_left = [left[base + k : base + k + 1, :] for k in range(GROUP)]
        row_right = [right[base + k : base + k + 1, :] for k in range(GROUP)]
        for k in range(GROUP):
            over = 1.0 / pivot[k][k]
            for m in range(k + 1, GROUP):
                factor = pivot[k][m] * over
                for n in range(m, GROUP):
                    pivot[m][n] = pivot[m][n] - factor * pivot[k][n]
                row_left[m] = row_left[m] - factor * row_left[k]
                row_right[m] = row_right[m] - factor * row_right[k]
                cols[m] = cols[m] - cols[k] * factor
            row_left[k] = row_left[k] * over
            row_right[k] = row_right[k] * over
        index = subs[: left.shape[0]]
        for k in range(GROUP):
            below = jnp.where(index > base + k, cols[k], 0.0)
            left = left - below * row_left[k]
            right = right - below * row_right[k]
        if base + GROUP == 8:
            top = first + GROUP - 8
            lane, sub = lanes[:8], subs[:8] + top
            diagonal = jnp.sum(jnp.where(lane == sub, left[:8], 0.0), axis=1, keepdims=True)
            over = 1.0 / jnp.sqrt(diagonal)
            upper[top : top + 8, :] = jnp.where(lane >= sub, left[:8] * over, 0.0)
            row = right[:8] * over
            inverse[top : top + 8, :] = row
            spread = spread + row * row * squares
            left, right = left[8:], right[8:]
    growth[0, 0] = jnp.sum(spread) * (1.0 / size)


def scatter_kernel(
    share, block, out, whole, upper, inverse, growth, own, got, far_in, near_in, pair, cross_in, last, z_in, part, got_narrow, mid, got_z, both,
    so, sc, rc, sf, rf, sn, rn, sb, rb, sz, rz, *gram_sems,
):
    x, y, z, core = place()
    other = 1 - core
    f32, bf16 = jnp.float32, jnp.bfloat16
    gram = gram_steps(part, whole, got_narrow, mid, got_z, both, *gram_sems)

    def along(kind, step):
        if kind == 0:
            return at((x + step) % NX, y, z, core)
        return at(x, (y + step) % NY, z, core)

    def chunk(ref, kind, duo, step):
        if kind == 0:
            return ref.at[2 * duo, (x + step) % NX]
        return ref.at[2 * duo + 1, :, (y + step) % NY]

    def half_of(ref, kind, duo, step, half):
        if kind == 0:
            return ref.at[2 * duo, (x + step) % NX, pl.ds(2 * half, 2)]
        return ref.at[2 * duo + 1, pl.ds(2 * half, 2), (y + step) % NY]

    def line(ref, kind, duo, step, index):
        if kind == 0:
            return ref.at[2 * duo, (x + step) % NX, index]
        return ref.at[2 * duo + 1, index, (y + step) % NY]

    mine = pltpu.make_async_copy(share.at[core], own, so)

    def across(kind, duo, step):
        source, target = chunk(share.at[other], kind, duo, step), chunk(got, kind, duo, step)
        return remote(source, target, sc.at[kind, duo, step], rc.at[kind, duo, step], at(x, y, z, other))

    def far(kind, duo, side):
        source = half_of(own, kind, duo, 2, side)
        return remote(
            source, far_in.at[kind, duo, side], sf.at[kind, duo, side], rf.at[kind, duo, side],
            along(kind, 3 if side else 1),
        )

    def near(kind, duo, side, half):
        step = 3 if side else 1
        source = half_of(own, kind, duo, step, half)
        target = near_in.at[kind, duo, side, pl.ds(2 * half, 2)]
        return remote(
            source, target, sn.at[kind, duo, side, half], rn.at[kind, duo, side, half], along(kind, step)
        )

    def cross(kind, duo, k):
        to = (y + k) % NY if kind == 0 else (x + k) % NX
        return remote(
            pair.at[kind, duo, to], cross_in.at[kind, duo, k - 1], sb.at[kind, duo, k], rb.at[kind, duo, k],
            along(1 - kind, k),
        )

    def third(duo, k):
        to = (z + k) % NZ
        return remote(
            last.at[duo, to], z_in.at[duo, k - 1], sz.at[duo, k], rz.at[duo, k], at(x, y, to, core)
        )

    order = (2, 1, 3, 0)

    def send_over(duo):
        for step in order:
            for kind in range(2):
                across(kind, duo, step).start()

    def join(kind, duo, step):
        across(kind, duo, step).wait_recv()

        def add(index):
            a, b = line(own, kind, duo, step, index), line(got, kind, duo, step, index)
            a[...] = (a[...].astype(f32) + b[...].astype(f32)).astype(bf16)

        loop(0, 4, add)

    def first_far(duo):
        for kind in range(2):
            join(kind, duo, 2)
            far(kind, duo, 0).start()
            far(kind, duo, 1).start()

    def first_near(duo):
        for kind in range(2):
            for side in range(2):
                join(kind, duo, 3 if side else 1)
                near(kind, duo, side, 1 - side).start()
        for kind in range(2):
            for side in range(2):
                far(kind, duo, side).wait_recv()

                def add(index):
                    a = line(own, kind, duo, 3 if side else 1, 2 * side + index)
                    a[...] = (a[...].astype(f32) + far_in[kind, duo, side, index].astype(f32)).astype(bf16)

                loop(0, 2, add)
                near(kind, duo, side, side).start()
        for kind in range(2):
            join(kind, duo, 0)

    def second(duo):
        for kind in range(2):
            for side in range(2):
                for half in range(2):
                    near(kind, duo, side, half).wait_recv()

            def add(index):
                total = line(own, kind, duo, 0, index)[...].astype(f32)
                total = total + near_in[kind, duo, 0, index].astype(f32)
                total = total + near_in[kind, duo, 1, index].astype(f32)
                pair[kind, duo, index] = total.astype(bf16)

            loop(0, 4, add)
            loop(1, 4, lambda k: cross(kind, duo, k).start())

    def final(duo):
        for kind in range(2):
            loop(1, 4, lambda k: cross(kind, duo, k).wait_recv())

        def add(k):
            index = (z + k) % NZ
            for kind in range(2):
                total = pair[kind, duo, y if kind == 0 else x, index].astype(f32)
                for j in range(3):
                    total = total + cross_in[kind, duo, j, index].astype(f32)
                last[duo, index, kind] = total.astype(bf16)

        def send(k):
            add(k)
            third(duo, k).start()

        loop(0, 3, lambda k: send(4 - k))
        loop(5, NZ, send)
        send(1)
        add(0)

    def finish(duo):
        loop(1, NZ, lambda k: third(duo, k).wait_recv())
        total = last[duo, z].astype(f32)
        for k in range(NZ - 1):
            total = total + z_in[duo, k].astype(f32)
        out[duo] = total

    def drain_first(duo):
        for kind in range(2):
            loop(0, 4, lambda step: across(kind, duo, step).wait_send())
            for side in range(2):
                far(kind, duo, side).wait_send()

    def drain_second(duo):
        for kind in range(2):
            for side in range(2):
                for half in range(2):
                    near(kind, duo, side, half).wait_send()
            loop(1, 4, lambda k: cross(kind, duo, k).wait_send())

    mine.start()
    gram.hail()
    part[...] = jnp.zeros_like(part)

    def add_gram(step):
        total = part[...]
        for u in range(4):
            rows = block[step * 4 + u]
            total = total + lax.dot_general(
                rows, rows, (((0,), (0,)), ((), ())), precision=precise, preferred_element_type=f32
            )
        part[...] = total

    loop(0, RB_DEV // 4, add_gram)
    gram.greet()
    loop(0, 2, send_over)
    mine.wait()
    first_far(0)
    gram.scatter_start()
    first_near(0)
    first_far(1)
    first_near(1)
    gram.scatter_finish()
    gram.exchange_finish()
    second(0)
    gram.across_finish()
    second(1)
    loop(0, 2, drain_first)
    gram.drain_early()
    loop(0, 2, final)
    loop(0, 2, drain_second)
    gram.spread_finish()
    factor_into(whole, upper, inverse, growth)
    loop(0, 2, finish)
    loop(0, 2, lambda duo: loop(1, NZ, lambda k: third(duo, k).wait_send()))


def scatter_shares(share, block, collective_id):
    width = share.shape[-1]
    bf16 = jnp.bfloat16
    dma = pltpu.SemaphoreType.DMA
    tail = (NZ, QUARTER, width)
    vmem = pltpu.VMEM
    in_vmem = pl.BlockSpec(memory_space=pltpu.VMEM)
    square = jax.ShapeDtypeStruct((width, width), jnp.float32)
    summed, *factored = pl.pallas_call(
        scatter_kernel,
        out_shape=(
            jax.ShapeDtypeStruct((2, 2, QUARTER, width), jnp.float32),
            square,
            square,
            square,
            jax.ShapeDtypeStruct((1, 1), jnp.float32),
        ),
        in_specs=[pl.BlockSpec(memory_space=pl.ANY), in_vmem],
        out_specs=(in_vmem, in_vmem, in_vmem, in_vmem, pl.BlockSpec(memory_space=pltpu.SMEM)),
        scratch_shapes=[
            vmem((4, NX, NY, *tail), bf16),
            vmem((4, NX, NY, *tail), bf16),
            vmem((2, 2, 2, 2, *tail), bf16),
            vmem((2, 2, 2, 4, *tail), bf16),
            vmem((2, 2, 4, *tail), bf16),
            vmem((2, 2, 3, *tail), bf16),
            vmem((2, NZ, 2, QUARTER, width), bf16),
            vmem((2, NZ - 1, 2, QUARTER, width), bf16),
            vmem(square.shape, jnp.float32),
            *gram_buffers(square),
            dma,
            dma((2, 2, 4)),
            dma((2, 2, 4)),
            dma((2, 2, 2)),
            dma((2, 2, 2)),
            dma((2, 2, 2, 2)),
            dma((2, 2, 2, 2)),
            dma((2, 2, 4)),
            dma((2, 2, 4)),
            dma((2, NZ)),
            dma((2, NZ)),
            *gram_semaphores(),
        ],
        compiler_params=pltpu.CompilerParams(
            collective_id=collective_id, has_side_effects=True, vmem_limit_bytes=VMEM_LIMIT
        ),
        name="scatter_shares",
    )(share, block)
    return summed.reshape(4 * QUARTER, width), *factored


UNROLL = 16


def slab_kernel(
    columns, rows, count, values_hbm, omega_hbm, sketch, share,
    values, omega, blank, totals, packed, rounded, seen, first, sv, so, sb, sw,
):
    live = count[0]
    steps = (live + UNROLL - 1) // UNROLL
    bring_values = pltpu.make_async_copy(values_hbm, values, sv)

    def bring(slot):
        core, x, y, z = column_place(columns[slot])
        return pltpu.make_async_copy(omega_hbm.at[core, :, x, y, z], omega.at[slot], so.at[slot])

    bring_values.start()
    loop(0, live, lambda slot: bring(slot).start())

    def clear(x):
        blank[x] = jnp.zeros(blank.shape[1:], jnp.bfloat16)

    loop(0, NX, clear)

    def wipe(core, quarter):
        return pltpu.make_async_copy(blank, share.at[core, quarter], sb.at[core, quarter])

    for core in range(2):
        for quarter in range(4):
            wipe(core, quarter).start()
    sketch[...] = jnp.zeros_like(sketch)

    def unseen(step):
        for u in range(8):
            seen[step * 8 + u] = -1

    loop(0, seen.shape[0] // 8, unseen)

    def number(slot):
        first[slot] = slot

    loop(live, steps * UNROLL, number)

    def look(slot):
        before = seen[columns[slot]]
        chosen = jnp.where(before < 0, slot, before)
        seen[columns[slot]] = chosen
        first[slot] = chosen

    loop(0, live, look)
    loop(0, live, lambda slot: bring(slot).wait())
    bring_values.wait()

    def add_sketch(step):
        products = []
        for u in range(UNROLL):
            slot = step * UNROLL + u
            picked = omega[slot].reshape(BLOCK, omega.shape[-1])
            products.append(jnp.dot(values[slot], picked, preferred_element_type=jnp.float32))
        for u in range(UNROLL):
            slot = step * UNROLL + u
            row = rows[slot] % RB_DEV
            sketch[row] = sketch[row] + jnp.where(slot < live, products[u], 0.0)

    loop(0, steps, add_sketch)
    rounded[...] = sketch[...].astype(jnp.bfloat16)

    def add_share(step):
        products = []
        for u in range(UNROLL):
            slot = step * UNROLL + u
            products.append(
                lax.dot_general(
                    values[slot],
                    rounded[rows[slot] % RB_DEV],
                    (((0,), (0,)), ((), ())),
                    preferred_element_type=jnp.float32,
                )
            )
        for u in range(UNROLL):
            slot = step * UNROLL + u
            target = first[slot]
            totals[target] = jnp.where(target == slot, 0.0, totals[target]) + products[u]

    loop(0, steps, add_share)
    for core in range(2):
        for quarter in range(4):
            wipe(core, quarter).wait()

    def hand_out(slot):
        core, x, y, z = column_place(columns[slot])
        return pltpu.make_async_copy(packed.at[slot], share.at[core, :, x, y, z], sw.at[slot])

    def pack(step):
        for u in range(UNROLL):
            slot = step * UNROLL + u
            packed[slot] = totals[slot].astype(jnp.bfloat16).reshape(packed.shape[1:])
        for u in range(UNROLL):
            slot = step * UNROLL + u

            @pl.when((first[slot] == slot) & (slot < live))
            def _():
                hand_out(slot).start()

    loop(0, steps, pack)

    def done(slot):
        @pl.when(first[slot] == slot)
        def _():
            hand_out(slot).wait()

    loop(0, live, done)


def slab_products(values, columns, rows, count, omega):
    slots = values.shape[0]
    width = omega.shape[-1]
    smem = pl.BlockSpec(memory_space=pltpu.SMEM)
    vmem = pl.BlockSpec(memory_space=pltpu.VMEM)
    hbm = pl.BlockSpec(memory_space=pl.ANY)
    dma = pltpu.SemaphoreType.DMA
    f32, bf16 = jnp.float32, jnp.bfloat16
    return pl.pallas_call(
        slab_kernel,
        out_shape=(
            jax.ShapeDtypeStruct((RB_DEV, BLOCK, width), f32),
            jax.ShapeDtypeStruct((2, 4, NX, NY, NZ, QUARTER, width), bf16),
        ),
        in_specs=[smem, smem, smem, hbm, hbm],
        out_specs=(vmem, hbm),
        scratch_shapes=[
            pltpu.VMEM(values.shape, bf16),
            pltpu.VMEM((slots, 4, QUARTER, width), bf16),
            pltpu.VMEM((NX, NY, NZ, QUARTER, width), bf16),
            pltpu.VMEM((slots, BLOCK, width), f32),
            pltpu.VMEM((slots, 4, QUARTER, width), bf16),
            pltpu.VMEM((RB_DEV, BLOCK, width), bf16),
            pltpu.SMEM((NCOL // BLOCK,), jnp.int32),
            pltpu.SMEM((slots,), jnp.int32),
            dma,
            dma((slots,)),
            dma((2, 4)),
            dma((slots,)),
        ],
        compiler_params=pltpu.CompilerParams(vmem_limit_bytes=VMEM_LIMIT),
        name="slab_products",
    )(columns, rows, count, values, omega)


def project_kernel(columns, rows, count, values, basis, out, total):
    live = count[0]

    def clear(step):
        for core in range(2):
            for quarter in range(4):
                total[core, quarter, step // NY, step % NY] = jnp.zeros(total.shape[4:], jnp.float32)

    loop(0, NX * NY, clear)

    def some(step):
        for u in range(UNROLL):
            slot = step * UNROLL + u
            core, x, y, z = column_place(columns[slot])
            product = lax.dot_general(
                values[slot], basis[rows[slot] % RB_DEV], (((0,), (0,)), ((), ())), preferred_element_type=jnp.float32
            )
            product = jnp.where(slot < live, product, 0.0)
            for quarter in range(4):
                piece = product[quarter * QUARTER : (quarter + 1) * QUARTER]
                total[core, quarter, x, y, z] = total[core, quarter, x, y, z] + piece

    loop(0, (live + UNROLL - 1) // UNROLL, some)

    def narrow(step):
        x, y = step // NY, step % NY
        for core in range(2):
            for quarter in range(4):
                out[core, quarter, x, y] = total[core, quarter, x, y].astype(jnp.bfloat16)

    loop(0, NX * NY, narrow)


def project_slab(values, columns, rows, count, basis):
    width = basis.shape[-1]
    smem = pl.BlockSpec(memory_space=pltpu.SMEM)
    vmem = pl.BlockSpec(memory_space=pltpu.VMEM)
    shape = (2, 4, NX, NY, NZ, QUARTER, width)
    return pl.pallas_call(
        project_kernel,
        out_shape=jax.ShapeDtypeStruct(shape, jnp.bfloat16),
        in_specs=[smem, smem, smem, vmem, vmem],
        out_specs=vmem,
        scratch_shapes=[pltpu.VMEM(shape, jnp.float32)],
        compiler_params=pltpu.CompilerParams(vmem_limit_bytes=VMEM_LIMIT),
        name="project_slab",
    )(columns, rows, count, values, basis)


def full_dot(left, right, contract):
    return lax.dot_general(
        left, right, ((contract[:1], contract[1:]), ((), ())), precision=precise, preferred_element_type=jnp.float32
    )


def right_divide(row_block, lower_part):
    return lax.linalg.triangular_solve(
        lower_part, row_block, left_side=False, lower=True, transpose_a=True
    )


GROWTH_LIMIT = 2.0


def on_device(block_values, block_rows, block_cols, block_count, test_matrix):
    slot_count, width_block, _ = block_values.shape
    sketch_width = test_matrix.shape[1]
    slab_total = lax.axis_size("wide") * lax.axis_size("narrow")
    omega = gather_rows(test_matrix)
    blocks, share = slab_products(block_values, block_cols, block_rows, block_count, omega)
    sketch = blocks.reshape(RB_DEV * width_block, sketch_width)
    total_rows = sketch.shape[0] * slab_total
    row_scale = math.sqrt(total_rows)
    column_scale = math.sqrt(NCOL / (slot_count * slab_total * width_block))
    summed, whole, upper, inverse, growth = scatter_shares(share, blocks, 1)

    def one_pass(sketch, summed, whole, upper, inverse):
        q_basis = (full_dot(sketch, inverse, (1, 1)) * row_scale).astype(jnp.bfloat16)
        projected = full_dot(summed, inverse, (1, 1)) * (row_scale * column_scale)
        return q_basis, upper / row_scale, projected

    def two_passes(sketch, summed, whole, upper, inverse):
        lower_one = jnp.linalg.cholesky(whole)
        first_basis = right_divide(sketch, lower_one)
        second_gram = full_dot(first_basis, first_basis, (0, 0))
        lower_two = jnp.linalg.cholesky(total_over_devices(second_gram, 2))
        q_basis = (right_divide(first_basis, lower_two) * row_scale).astype(jnp.bfloat16)
        r_factor = full_dot(lower_one, lower_two, (1, 0)).T / row_scale
        basis_blocks = q_basis.reshape(RB_DEV, width_block, sketch_width)
        basis_share = project_slab(block_values, block_cols, block_rows, block_count, basis_blocks)
        projected, *_ = scatter_shares(
            basis_share, first_basis.reshape(RB_DEV, width_block, sketch_width), 3
        )
        return q_basis, r_factor, projected * column_scale

    return lax.cond(
        growth[0, 0] <= GROWTH_LIMIT, one_pass, two_passes, sketch, summed, whole, upper, inverse
    )


def solution(mesh):
    placed = (
        P(AXES, None, None),
        P(AXES),
        P(AXES),
        P(AXES),
        P(AXES, None),
    )
    return jax.shard_map(
        on_device,
        mesh=mesh,
        in_specs=placed,
        out_specs=(P(AXES, None), P(), P(AXES, None)),
        check_vma=False,
    )
```
